128 devices in a mesh: gx: 8 (over x, core), gy: 16 (over y, z).
Axes of the slice: x: 4, y: 4, z: 4, core: 2. Of those that a mesh axis runs over, the one named last changes fastest.
Arguments:
- fine_in: bfloat16 [8192, 64, 512], P(('gx', 'gy')), may hold values from -10 to 10
- neighbours: int32 [8192, 6], P(('gx', 'gy')), may hold values from -1 to 8191, as said below
- parent_dev: int32 [8192, 1], P(('gx', 'gy')), may hold values from 0 to 127; in each aligned block of 64 rows (0 to 63, 64 to 127, ...) at most 2 rows name the same one
- parent_cell: int32 [8192], P(('gx', 'gy')), may hold values from 0 to 127
- timestep: int32 [1], replicated, may hold values from 0 to 999
- conv_weight: bfloat16 [7, 64, 64], replicated, may hold values from -0.25 to 0.25
- time_weight: float32 [64, 64], replicated, may hold values from -0.75 to 0.75
- up_weight: bfloat16 [64, 256], replicated, may hold values from -0.75 to 0.75
- coarse_in: bfloat16 [128, 128, 256], P('gx', 'gy'), may hold values from -6 to 6
- coarse_kernel: bfloat16 [9, 256, 256], replicated, may hold values from -0.125 to 0.125
- out_weight: bfloat16 [256, 256], replicated, may hold values from -0.375 to 0.375
- coarse_cot: bfloat16 [128, 128, 256], P('gx', 'gy'), may hold values from -6 to 6
Outputs:
- fine_act: bfloat16 [8192, 64, 512], P(('gx', 'gy'))
- coarse_out: bfloat16 [128, 128, 256], P('gx', 'gy')
- grad_conv: float32 [7, 64, 64], replicated
- grad_time: float32 [64, 64], replicated
- grad_up: float32 [64, 256], replicated
- grad_kernel: float32 [9, 256, 256], replicated
- grad_out: float32 [256, 256], replicated
The draws below stay inside these ranges and needn't reach their ends.
Inputs may be any that keep to these rules, and one draw needn't show every extreme that they name: An entry is a brick number or -1 for no neighbour. The lists are symmetric: neighbours[n, f] = j >= 0 exactly when neighbours[j, g] = n, with g the face opposite to f (f xor 1). Brick n lies on device n // 64 of gx+gy. An entry of face 2 k of a brick on device i (k = 0, 1, 2) names a brick of device i or of device (i + d) modulo the device count, and an entry of face 2 k + 1 one of device i or (i - d) modulo the device count, with d in k * 2 + 1 .. (k + 1) * 2. For each face and each such d, exactly 12 entries of one device's bricks name bricks of that other device. `parent_dev`: among the 64 bricks of one device at most 2 have the same value, and some device reaches that.
All inputs are finite; a program needn't handle non-finite values.
Results may differ from the reference program's by a relative error of at most 0.0075.
Values may be sent and summed in bfloat16 or wider, within the bound.
A program may use at most 256 MiB of HBM per device.

```python
import math
import jax
import jax.numpy as jnp
import numpy as np
from jax import lax

CH = 64
CW = 256
VOX = 512
BD = 64
KOFF = 2
MFACE = 12
CTX = 16
CTY = 8
PCAP = 2
NBRICK = 8192
NCX = 128
NCY = 128
N_GX = 8
N_GY = 16


def draw_fine_in(key, part):
    key = jax.random.fold_in(key, 5)
    first, second = jax.random.split(key, 2)
    noise = jax.random.normal(first, (NBRICK, CH, VOX), jnp.float32)
    centre = jax.random.normal(second, (NBRICK, CH, 1), jnp.float32)
    return jnp.clip(noise + centre, -10.0, 10.0).astype(jnp.bfloat16)


def draw_neighbours(key, part):
    key = jax.random.fold_in(key, 11)
    device_count = NBRICK // BD
    streams = jax.random.split(key, 4)
    offsets = (jnp.arange(3 * KOFF, dtype=jnp.int32) + 1).reshape(3, KOFF)
    brick = jnp.arange(NBRICK, dtype=jnp.int32)
    device = brick // BD
    within = brick % BD
    columns = []
    for axis_number in range(3):
        first, second, third = jax.random.split(streams[axis_number + 1], 3)
        position = jax.random.permutation(first, BD).astype(jnp.int32)
        group = jnp.minimum(position // MFACE, KOFF - 1)
        distance = jnp.where(position < KOFF * MFACE, offsets[axis_number][group], 0).astype(jnp.int32)
        orders = jax.vmap(lambda single: jax.random.permutation(single, BD))(jax.random.split(second, device_count)).astype(jnp.int32)
        inverse = jnp.argsort(orders, axis=1).astype(jnp.int32)
        keeping = jax.random.randint(third, (NBRICK,), 0, 4) > 0
        source_distance = distance[within]
        target_device = (device + source_distance) % device_count
        forward = target_device * BD + orders[target_device, within]
        plus_side = jnp.where(keeping | (source_distance != 0), forward, -1)
        anchor_slot = inverse[device, within]
        anchor_distance = distance[anchor_slot]
        anchor_device = (device - anchor_distance) % device_count
        backward = anchor_device * BD + anchor_slot
        minus_side = jnp.where(keeping[backward] | (anchor_distance != 0), backward, -1)
        columns.append(plus_side)
        columns.append(minus_side)
    return jnp.stack(columns, axis=1).astype(jnp.int32)


def set_ends(values, own_key, smallest, top_value):
    longest = values.shape.index(max(values.shape))
    spots = []
    for shift in (0, 1):
        where = [jax.random.randint(jax.random.fold_in(own_key, axis), (), 0, length) for axis, length in enumerate(values.shape)]
        where[longest] = (where[longest] + shift) % values.shape[longest]
        spots.append(tuple(where))
    return values.at[spots[0]].set(smallest).at[spots[1]].set(top_value)


def steps_of(stream_key, extent, cuts, smallest, largest):
    def one(axis_at, blocks):
        heights = jax.random.uniform(jax.random.fold_in(jax.random.fold_in(stream_key, 6), axis_at), (blocks,), jnp.float32, smallest / len(cuts), largest / len(cuts))
        return jnp.repeat(jnp.exp(heights), extent[axis_at] // blocks).reshape((-1,) + (1,) * (len(extent) - axis_at - 1))

    factor_of = one(*cuts[0])
    for cut in cuts[1:]:
        factor_of = factor_of * one(*cut)
    return factor_of


def assign_block(key, own, number, rows, amount, top, limit, lean):
    sequence = jax.random.permutation(key, amount)
    crowded, usual = portions_of(amount, rows * top, limit, lean, True), portions_of(amount, rows * top, limit, lean, False)
    places = jnp.arange(amount)

    def named(tallies, rotation):
        used = int((tallies > 0).sum())
        fixed = max(1, used // 4)
        passed = fixed + (places - fixed + rotation * (used - fixed)) % max(1, amount - fixed)
        return jnp.zeros((amount,), jnp.int32).at[sequence[jnp.where(places < fixed, places, passed)]].set(jnp.asarray(tallies, jnp.int32))

    tallies = jnp.where(number % 4 == 0, named(crowded, number // 4), named(usual, number - number // 4 - 1))
    mixed = jax.random.permutation(jax.random.fold_in(own, 3), amount)
    source_of, taker = mixed[0:amount // 2 * 2:2], mixed[1:amount // 2 * 2:2]
    room = jnp.minimum(tallies[source_of] - 1, limit - tallies[taker]) // 2
    room = jnp.where((source_of == sequence[0]) | (taker == sequence[0]) | (tallies[taker] == 0), 0, jnp.maximum(room, 0))
    passed = jax.random.randint(jax.random.fold_in(own, 4), (amount // 2,), 0, 1 << 20) % (room + 1)
    tallies = tallies.at[source_of].add(-passed).at[taker].add(passed)
    items = jnp.searchsorted(jnp.cumsum(tallies), jnp.arange(rows * top), side="right").astype(jnp.int32)
    grid = items.reshape(top, rows).T
    grid = grid[jax.random.permutation(jax.random.fold_in(own, 1), rows)]
    rotation = jax.random.randint(jax.random.fold_in(own, 2), (rows, 1), 0, top)
    return jnp.take_along_axis(grid, (jnp.arange(top)[None, :] + rotation) % top, axis=1)


def portions_of(amount, total, most, skew, full):
    portions = [(1 << 20) // math.isqrt(grade ** skew) + 1 for grade in range(1, amount + 1)]
    largest = most if full else min(most, max(-(-total // amount), total * portions[0] // sum(portions)))
    least = 1 if total - largest >= amount - 1 else 0
    given, surplus = [largest] + [least] * (amount - 1), total - largest - least * (amount - 1)
    while surplus > 0:
        candidates = [i for i in range(1, amount) if given[i] < largest] or [i for i in range(1, amount) if given[i] < most]
        pool, remaining = sum([portions[i] for i in candidates]), surplus
        for i in candidates:
            more = min(most - given[i], max(1, remaining * portions[i] // pool), surplus)
            given[i] = given[i] + more
            surplus = surplus - more
    return np.array(given)


def centred(key, shape, spread, bound, cuts=(), kind=jnp.bfloat16):
    entries = jax.random.normal(key, shape, jnp.float32) * spread
    if len(cuts) > 0:
        entries = steps_of(key, shape, cuts, -0.22, 0.18) * entries
    return jnp.clip(entries, min=-bound, max=bound).astype(kind)


def setup_inputs(seed: int = 0) -> dict:
    streams_of = jax.random.split(jax.random.key(seed), 13)
    fine_in = draw_fine_in(jax.random.fold_in(streams_of[12], 71), 0)
    neighbours = draw_neighbours(jax.random.fold_in(streams_of[12], 71), 0)
    parent_dev_keys = jax.random.split(jax.random.fold_in(streams_of[2], 1), NBRICK // BD)
    parent_dev_turns = jax.random.permutation(jax.random.fold_in(streams_of[2], 3), NBRICK // BD)
    parent_dev = jax.vmap(lambda own, number: assign_block(jax.random.fold_in(streams_of[2], 2), own, number, BD, N_GX * N_GY, 1, PCAP, 2))(parent_dev_keys, parent_dev_turns).reshape((NBRICK, 1))
    parent_cell = set_ends(jax.random.randint(streams_of[3], (NBRICK,), 0, CTX * CTY), jax.random.fold_in(streams_of[3], 1), 0, (CTX * CTY) - 1).astype(jnp.int32)
    timestep = jax.random.randint(streams_of[4], (1,), 0, 1000).astype(jnp.int32)
    conv_weight = centred(streams_of[5], (7, CH, CH), (7 * CH) ** -0.5, 0.25)
    time_weight = centred(streams_of[6], (CH, CH), CH ** -0.5, 0.75, (), jnp.float32)
    up_weight = centred(streams_of[7], (CH, CW), CH ** -0.5, 0.75)
    coarse_in = centred(streams_of[8], (NCX, NCY, CW), 1.0, 6.0, ((0, 8), (1, 16)))
    coarse_kernel = centred(streams_of[9], (9, CW, CW), (9 * CW) ** -0.5, 0.125)
    out_weight = centred(streams_of[10], (CW, CW), CW ** -0.5, 0.375)
    coarse_cot = centred(streams_of[11], (NCX, NCY, CW), 1.0, 6.0, ((0, 8), (1, 16)))
    return {"fine_in": fine_in, "neighbours": neighbours, "parent_dev": parent_dev, "parent_cell": parent_cell, "timestep": timestep, "conv_weight": conv_weight, "time_weight": time_weight, "up_weight": up_weight, "coarse_in": coarse_in, "coarse_kernel": coarse_kernel, "out_weight": out_weight, "coarse_cot": coarse_cot}


def time_features(timestep, channels):
    half_count = channels // 2
    frequency = jnp.exp(-math.log(10000.0) * jnp.arange(half_count, dtype=jnp.float32) / half_count)
    angles = timestep[0].astype(jnp.float32) * frequency
    return jnp.concatenate([jnp.sin(angles), jnp.cos(angles)])

def silu_grad(values):
    sigma = jax.nn.sigmoid(values)
    return sigma * (1.0 + values * (1.0 - sigma))

def face_planes(field):
    bricks, channels, voxels = field.shape
    volume = field.reshape(bricks, channels, 8, 8, 8)
    faces_list = [volume[:, :, 7], volume[:, :, 0], volume[:, :, :, 7], volume[:, :, :, 0], volume[:, :, :, :, 7], volume[:, :, :, :, 0]]
    return jnp.stack(faces_list, axis=1).reshape(bricks, 6, channels * 64)

def spread_plane(face_plane, missing):
    bricks, channels = (face_plane.shape[0], face_plane.shape[1])
    if missing == 1:
        shaped = face_plane.reshape(bricks, channels, 8, 1, 8)
    else:
        shaped = face_plane.reshape(bricks, channels, 8, 8, 1)
    return jnp.broadcast_to(shaped, (bricks, channels, 8, 8, 8)).reshape(bricks, channels, 512)

def shifted_stack(field, nearby):
    voxels = field.shape[2]
    position = jnp.arange(voxels)
    index_y = position // 8 % 8
    index_z = position % 8
    zeros_eight = jnp.zeros_like(field[..., :8])
    zeros_one = jnp.zeros_like(field[..., :1])
    plus_x = jnp.concatenate([field[..., 64:], nearby[:, 0]], axis=-1)
    minus_x = jnp.concatenate([nearby[:, 1], field[..., :voxels - 64]], axis=-1)
    plus_y = jnp.where(index_y == 7, spread_plane(nearby[:, 2], 1), jnp.concatenate([field[..., 8:], zeros_eight], axis=-1))
    minus_y = jnp.where(index_y == 0, spread_plane(nearby[:, 3], 1), jnp.concatenate([zeros_eight, field[..., :voxels - 8]], axis=-1))
    plus_z = jnp.where(index_z == 7, spread_plane(nearby[:, 4], 2), jnp.concatenate([field[..., 1:], zeros_one], axis=-1))
    minus_z = jnp.where(index_z == 0, spread_plane(nearby[:, 5], 2), jnp.concatenate([zeros_one, field[..., :voxels - 1]], axis=-1))
    return jnp.stack([field, plus_x, minus_x, plus_y, minus_y, plus_z, minus_z], axis=0)

def reference(fine_in, neighbours, parent_dev, parent_cell, timestep, conv_weight, time_weight, up_weight, coarse_in, coarse_kernel, out_weight, coarse_cot):
    highest = lax.Precision.HIGHEST
    device_count = N_GX * N_GY
    time_basis = time_features(timestep, CH)
    embedding = jnp.dot(time_weight, time_basis, precision=highest)
    planes_all = face_planes(fine_in)
    facing = jnp.arange(6, dtype=jnp.int32)
    opposite = facing + 1 - 2 * (facing % 2)

    def gather_near(block_nb):
        safe_index = jnp.maximum(block_nb, 0).astype(jnp.int32)
        fetched = planes_all[safe_index, opposite[None, :]]
        fetched = jnp.where((block_nb >= 0)[:, :, None], fetched, jnp.zeros_like(fetched))
        return fetched.reshape(block_nb.shape[0], 6, CH, 64)

    def block_hidden(block_in, block_nb):
        stacked = shifted_stack(block_in, gather_near(block_nb))
        hidden = jnp.einsum('foc,fbcv->bov', conv_weight.astype(jnp.float32), stacked.astype(jnp.float32), precision=highest)
        return (stacked, hidden + embedding[None, :, None])

    def forward_block(inputs):
        block_in, block_nb = inputs
        stacked, hidden = block_hidden(block_in, block_nb)
        activated = jax.nn.silu(hidden)
        return (activated.astype(jnp.bfloat16), lax.optimization_barrier(jnp.mean(activated, axis=-1)).astype(jnp.bfloat16))
    fine_blocks = fine_in.reshape(device_count, BD, CH, VOX)
    nb_blocks = neighbours.reshape(device_count, BD, 6)
    fine_act, pooled = lax.map(forward_block, (fine_blocks, nb_blocks))
    fine_act = fine_act.reshape(NBRICK, CH, VOX)
    pooled = pooled.reshape(NBRICK, CH)
    lifted = jnp.dot(pooled, up_weight, preferred_element_type=jnp.float32).astype(jnp.bfloat16)
    owners = parent_dev[:, 0]
    row_cell = owners // N_GY * CTX + parent_cell // CTY
    col_cell = owners % N_GY * CTY + parent_cell % CTY
    injected = jnp.zeros((NCX, NCY, CW), jnp.float32).at[row_cell, col_cell].add(lifted.astype(jnp.float32))
    coarse_value = coarse_in.astype(jnp.float32)
    coarse_rim = jax.nn.silu(coarse_value).astype(jnp.bfloat16)
    padded = jnp.pad(coarse_rim, ((1, 1), (1, 1), (0, 0)))
    tap_rows = [padded[offset_row:offset_row + NCX, offset_col:offset_col + NCY].reshape(-1, CW) for offset_row in range(3) for offset_col in range(3)]
    convolved = jnp.zeros((NCX * NCY, CW), jnp.float32)
    for tap_index in range(9):
        convolved = convolved + jnp.dot(tap_rows[tap_index], coarse_kernel[tap_index], preferred_element_type=jnp.float32)
    coarse_pre = coarse_value.reshape(-1, CW) + convolved + injected.reshape(-1, CW)
    coarse_act = jax.nn.silu(coarse_pre).astype(jnp.bfloat16)
    coarse_out = (coarse_pre + jnp.dot(coarse_act, out_weight, preferred_element_type=jnp.float32)).astype(jnp.bfloat16).reshape(NCX, NCY, CW)
    loss_scale = 1.0 / math.sqrt(NCX * NCY)
    grad_outs = (coarse_cot.astype(jnp.float32).reshape(-1, CW) * loss_scale).astype(jnp.bfloat16)
    through = jnp.dot(grad_outs, out_weight.T, preferred_element_type=jnp.float32)
    grad_pre = (grad_outs.astype(jnp.float32) + through * silu_grad(coarse_pre)).astype(jnp.bfloat16)
    grad_out = jnp.dot(coarse_act.T, grad_outs, preferred_element_type=jnp.float32)
    grad_kernel = jnp.stack([jnp.dot(tap_rows[tap_index].T, grad_pre, preferred_element_type=jnp.float32) for tap_index in range(9)])
    grad_grid = grad_pre.reshape(NCX, NCY, CW)
    grad_lifted = grad_grid[row_cell, col_cell]
    grad_up = jnp.dot(pooled.T, grad_lifted, preferred_element_type=jnp.float32)
    grad_pooled = jnp.dot(grad_lifted, up_weight.T, preferred_element_type=jnp.float32).astype(jnp.bfloat16)

    def backward_block(inputs):
        block_in, block_nb, block_grad = inputs
        stacked, hidden = block_hidden(block_in, block_nb)
        grad_hidden = block_grad.astype(jnp.float32)[:, :, None] / VOX * silu_grad(hidden)
        grad_hidden_low = grad_hidden.astype(jnp.bfloat16)
        block_conv = jnp.einsum('bov,fbcv->foc', grad_hidden_low.astype(jnp.float32), stacked.astype(jnp.float32), precision=highest)
        return (block_conv, lax.optimization_barrier(jnp.sum(grad_hidden, axis=(0, 2))))
    conv_parts, time_parts = lax.map(backward_block, (fine_blocks, nb_blocks, grad_pooled.reshape(device_count, BD, CH)))
    grad_conv = lax.optimization_barrier(jnp.sum(conv_parts, axis=0))
    grad_time = jnp.outer(lax.optimization_barrier(jnp.sum(time_parts, axis=0)), time_basis)
    return (fine_act, coarse_out, grad_conv, grad_time, grad_up, grad_kernel, grad_out)
```

```python
import math

import jax
import jax.numpy as jnp
import numpy as np
from jax import lax
from jax.experimental import pallas as pl
from jax.experimental.pallas import tpu as pltpu
from jax.sharding import PartitionSpec as P

F32 = jnp.float32
BF16 = jnp.bfloat16
MESH = pl.DeviceIdType.MESH
NDEV = 128
NX = 8
NY = 16
BD = 64
CH = 64
VOX = 512
CW = 256
MFACE = 12
NBUCKET = 12
STEP = 8
TROWS = 464
GROWS = 5248
PAYLOAD = 6144
VMEM = pl.BlockSpec(memory_space=pltpu.VMEM)
SMEM = pl.BlockSpec(memory_space=pltpu.SMEM)

NN = (((1,), (0,)), ((), ()))
NT = (((1,), (1,)), ((), ()))


def mm(a, b, dims=NN):
    return lax.dot_general(a, b, dims, preferred_element_type=F32)


def sigmoid(u):
    return 0.5 * jnp.tanh(0.5 * u) + 0.5


def face_selector():
    table = np.zeros((VOX, 4 * 64), np.float32)
    for high in range(8):
        for low in range(8):
            place = 8 * high + low
            table[64 * high + 56 + low, place] = 1
            table[64 * high + low, 64 + place] = 1
            table[64 * high + 8 * low + 7, 128 + place] = 1
            table[64 * high + 8 * low, 192 + place] = 1
    return table


def face_spreader(table):
    out = np.zeros((4, 128, 2 * VOX), np.float32)
    for face in range(4):
        part = table[:, 64 * face : 64 * face + 64].T
        out[face, :64, :VOX] = part
        out[face, 64:, VOX:] = part
    return out


def bucket_offset(bucket):
    face, extra = bucket // 2, bucket % 2
    distance = 2 * (face // 2) + 1 + extra
    return distance if face % 2 == 0 else -distance


RIM_BLOCKS = (
    (0, 8, 1, 0),
    (8, 8, -1, 0),
    (16, 16, 0, 1),
    (32, 16, 0, -1),
    (48, 8, 1, 1),
    (56, 8, 1, -1),
    (64, 8, -1, 1),
    (72, 8, -1, -1),
)


def signal_all(me):
    barrier = pltpu.get_barrier_semaphore()

    def signal(step, carry):
        other = lax.rem(me + step, NDEV)
        pl.semaphore_signal(
            barrier, inc=1, device_id=(other // NY, lax.rem(other, NY)), device_id_type=MESH
        )
        return carry

    lax.fori_loop(1, NDEV, signal, 0)
    return barrier


def send_rows(me, src, dst, ssem, rsem):
    def send(step, carry):
        other = lax.rem(me + step, NDEV)
        pltpu.make_async_remote_copy(
            src_ref=src.at[pl.ds(2 * other, 2)],
            dst_ref=dst.at[pl.ds(2 * me, 2)],
            send_sem=ssem,
            recv_sem=rsem,
            device_id=(other // NY, lax.rem(other, NY)),
            device_id_type=MESH,
        ).start()
        return carry

    lax.fori_loop(1, NDEV, send, 0)
    dst[pl.ds(2 * me, 2)] = src[pl.ds(2 * me, 2)]
    other = lax.rem(me + 1, NDEV)
    every = pl.ds(0, 2 * (NDEV - 1))
    return pltpu.make_async_remote_copy(
        src_ref=src.at[every],
        dst_ref=dst.at[every],
        send_sem=ssem,
        recv_sem=rsem,
        device_id=(other // NY, lax.rem(other, NY)),
        device_id_type=MESH,
    )


def route_kernel(nb_ref, own_ref, index_ref, source_ref, slot_ref):
    me = lax.axis_index("gx") * NY + lax.axis_index("gy")
    square = jnp.concatenate(
        [nb_ref[...].astype(F32), own_ref[...].astype(F32), jnp.zeros((BD, 121), F32)], axis=1
    )
    flat = jnp.concatenate([square, square], axis=0).T.astype(jnp.int32)
    upper = lax.broadcasted_iota(jnp.int32, (BD, BD), 0)
    across = lax.broadcasted_iota(jnp.int32, (BD, BD), 1)
    earlier = upper < across
    slots = lax.broadcasted_iota(jnp.int32, (2 * MFACE, BD), 0)
    order = lax.broadcasted_iota(jnp.int32, (2 * MFACE, BD), 1)
    for face in range(6):
        facing = face + 1 - 2 * (face % 2)
        sign = 1 - 2 * (face % 2)
        row, column = flat[face : face + 1, :BD], nb_ref[:, face : face + 1]
        holder, holder_c = row >> 6, column >> 6
        local = row & 63
        present = row >= 0
        away = present & (holder != me)
        extra = ((sign * (holder - me) + NDEV) & (NDEV - 1)) - (2 * (face // 2) + 1)
        extra = jnp.clip(extra, 0, 1)
        alike = holder_c == holder
        rank_out = jnp.sum((alike & earlier).astype(jnp.int32), axis=0, keepdims=True)
        rank_in = jnp.sum((alike & (column < row)).astype(jnp.int32), axis=0, keepdims=True)
        place = jnp.where(away, extra * MFACE + jnp.minimum(rank_out, MFACE - 1), -1)
        found = jnp.sum(jnp.where(slots == place, order, 0), axis=1, keepdims=True)
        source_ref[:, face : face + 1] = found
        far = 6 * BD + facing * (2 * MFACE) + extra * MFACE + jnp.minimum(rank_in, MFACE - 1)
        near = facing * BD + local
        index_ref[face : face + 1] = jnp.where(away, far, jnp.where(present, near, 528))
    mine, mine_c = flat[6:7, :BD], own_ref[...]
    twin = jnp.sum(((mine == mine_c) & earlier).astype(jnp.int32), axis=0, keepdims=True)
    slot = mine * 2 + jnp.minimum(twin, 1)
    slot_ref[...] = jnp.concatenate([slot, jnp.full((1, BD), -1, jnp.int32)], axis=1)


def fine_kernel(
    src_ref, idx_ref, x_ref, sel_ref, spread_ref, cin_ref, cw_ref, tw_ref, basis_ref, slot_ref, cell_ref,
    fa_ref, tt_ref, rows_ref, rim_ref,
    own, planes, out_buf, rim_buf, shifted, slope, active_buf, tap_buf, near, spread, weight, pool, rows_buf,
    xsem, fsem, tsem, ssem, rsem, rows_ssem, rows_rsem,
):
    gx, gy = lax.axis_index("gx"), lax.axis_index("gy")
    me = gx * NY + gy
    loads = []
    for part in range(4):
        bricks = pl.ds(16 * part, 16)
        loads.append(
            pltpu.make_async_copy(x_ref.at[bricks], shifted.at[bricks, pl.ds(0, CH)], xsem.at[part])
        )
        loads[-1].start()
    barrier = signal_all(me)
    face_to = []
    for bucket in range(NBUCKET):
        other = lax.rem(me + bucket_offset(bucket) + NDEV, NDEV)
        face_to.append((other // NY, lax.rem(other, NY)))
    rim_to = [
        (lax.rem(gx + dx + NX, NX), lax.rem(gy + dy + NY, NY)) for _, _, dx, dy in RIM_BLOCKS
    ]

    rim = cin_ref[...].astype(F32)
    rim = (rim * sigmoid(rim)).astype(BF16).astype(F32)
    cube = rim.reshape(16, 8, CW)
    rim_buf[0:8] = cube[15]
    rim_buf[8:16] = cube[0]
    rim_buf[16:32] = cube[:, 7, :]
    rim_buf[32:48] = cube[:, 0, :]
    rim_buf[48:56] = jnp.broadcast_to(cube[15, 7:8], (8, CW))
    rim_buf[56:64] = jnp.broadcast_to(cube[15, 0:1], (8, CW))
    rim_buf[64:72] = jnp.broadcast_to(cube[0, 7:8], (8, CW))
    rim_buf[72:80] = jnp.broadcast_to(cube[0, 0:1], (8, CW))

    low = lax.broadcasted_iota(jnp.int32, (32, 128), 1) < 64

    def flip(values):
        return jnp.concatenate([values[:, 64:], values[:, :64]], axis=1)

    def pack(values, upper):
        top, bottom = values[:32], values[32:]
        if upper:
            return jnp.where(low, flip(top), bottom)
        return jnp.where(low, top, flip(bottom))

    def extract(group, carry):
        rows = shifted[pl.ds(group * 4, 4), 0:CH].reshape(4 * CH, VOX)
        picked = mm(rows, sel_ref[...]).astype(BF16)
        for b in range(4):
            n = group * 4 + b
            brick = rows[64 * b : 64 * b + 64]
            both = picked[64 * b : 64 * b + 64]
            for face, plane in enumerate(
                (
                    pack(brick[:, 384:], True),
                    pack(brick[:, :128], False),
                    pack(both[:, :128], False),
                    pack(both[:, :128], True),
                    pack(both[:, 128:], False),
                    pack(both[:, 128:], True),
                )
            ):
                own[face * BD + n] = plane
                planes[face * BD + n] = plane
        return carry

    for part in range(4):
        loads[part].wait()
        lax.fori_loop(4 * part, 4 * part + 4, extract, 0)
    planes[528:544] = jnp.zeros((16, 32, 128), BF16)

    pl.semaphore_wait(barrier, NDEV - 1)
    copies = []
    for face in range(6):

        def gather(slot, carry):
            out_buf[face * 2 * MFACE + slot] = own[face * BD + src_ref[slot, face]]
            return carry

        lax.fori_loop(0, 2 * MFACE, gather, 0)
        for bucket in (2 * face, 2 * face + 1):
            copies.append(
                pltpu.make_async_remote_copy(
                    src_ref=out_buf.at[pl.ds(bucket * MFACE, MFACE)],
                    dst_ref=planes.at[pl.ds(6 * BD + bucket * MFACE, MFACE)],
                    send_sem=ssem.at[bucket],
                    recv_sem=rsem.at[bucket],
                    device_id=face_to[bucket],
                    device_id_type=MESH,
                )
            )
            copies[-1].start()
    for number, (first, rows, _, _) in enumerate(RIM_BLOCKS):
        copies.append(
            pltpu.make_async_remote_copy(
                src_ref=rim_buf.at[pl.ds(first, rows)],
                dst_ref=rim_ref.at[pl.ds(first, rows)],
                send_sem=ssem.at[NBUCKET + number],
                recv_sem=rsem.at[NBUCKET + number],
                device_id=rim_to[number],
                device_id_type=MESH,
            )
        )
        copies[-1].start()

    weight[...] = jnp.concatenate([cw_ref[k] for k in range(7)], axis=1)
    pool[...] = jnp.zeros_like(pool)
    lane = lax.broadcasted_iota(jnp.int32, (CH, VOX), 1)
    by, bz = lane // 8 % 8, lane % 8
    keep = (by < 7, by > 0, bz < 7, bz > 0)
    tall_low = lax.broadcasted_iota(jnp.int32, (CH, 128), 1) < 64
    zero = jnp.zeros((CH, 128), BF16)

    def turned(values, shift):
        return jnp.concatenate([values[:, shift:], values[:, :shift]], axis=1)

    def shift_brick(n):
        field = shifted[n, 0:CH]
        flipped = turned(field, 64)
        shifted[n, 64:128, : VOX - 128] = flipped[:, : VOX - 128]
        shifted[n, 64:128, VOX - 128 :] = jnp.where(tall_low, flipped[:, VOX - 128 :], zero)
        back = turned(field, VOX - 64)
        shifted[n, 128:192, 128:] = back[:, 128:]
        shifted[n, 128:192, :128] = jnp.where(tall_low, zero, back[:, :128])
        for number, shift in enumerate((8, VOX - 8, 1, VOX - 1)):
            first = 192 + 64 * number
            moved = turned(field, shift)
            shifted[n, first : first + 64] = jnp.where(keep[number], moved, jnp.zeros_like(moved))
        shifted[n, 448:TROWS] = jnp.ones((16, VOX), BF16)

    def shift_two(pair, carry):
        shift_brick(2 * pair)
        shift_brick(2 * pair + 1)
        return carry

    lax.fori_loop(0, BD // 2, shift_two, 0)
    embed = jnp.sum(tw_ref[...] * basis_ref[...], axis=1, keepdims=True)
    pool_lane = lax.broadcasted_iota(jnp.int32, (CH, 128), 1)

    for copy in copies:
        copy.wait_recv()

    def fine_step(step, carry):
        for b in range(STEP):
            for face in range(6):
                near[face, 32 * b : 32 * b + 32] = planes[idx_ref[face, step * STEP + b]]
        for face in range(4):
            spread[face] = mm(near[2 + face], spread_ref[face]).astype(BF16)
        for b in range(STEP):
            n = step * STEP + b
            above, below = near[0, 32 * b : 32 * b + 32], near[1, 32 * b : 32 * b + 32]
            plus = jnp.concatenate([flip(above), above], axis=0)
            minus = jnp.concatenate([below, flip(below)], axis=0)
            shifted[n, 64:128, VOX - 128 :] += jnp.where(tall_low, zero, plus)
            shifted[n, 128:192, :128] += jnp.where(tall_low, minus, zero)
            for number in range(4):
                rows = spread[number, 32 * b : 32 * b + 32]
                first = 192 + 64 * number
                shifted[n, first : first + 32] += rows[:, :VOX]
                shifted[n, first + 32 : first + 64] += rows[:, VOX:]
            hidden = mm(weight[...], shifted[n, 0:448]) + embed
            sigma = sigmoid(hidden)
            active = hidden * sigma
            active_buf[n] = active.astype(BF16)
            mean = jnp.sum(active, axis=1, keepdims=True) * (1.0 / VOX)
            pool[0:64] += jnp.where(pool_lane == n, mean, 0.0)
            slope[n] = (sigma + active * (1.0 - sigma)).astype(BF16)
        return carry

    lax.fori_loop(0, BD // STEP, fine_step, 0)
    stored = pltpu.make_async_copy(active_buf, fa_ref, fsem)
    stored.start()

    pool[64:72] = jnp.broadcast_to(cell_ref[...], (8, 128))
    values = pool[...].astype(BF16)
    hot = (lax.broadcasted_iota(jnp.int32, (2 * NDEV, 128), 0) == slot_ref[...]).astype(BF16)
    rows_buf[...] = mm(hot, values, NT)[:, None, :]
    rows_moved = send_rows(me, rows_buf, rows_ref, rows_ssem, rows_rsem)

    def taps(pair, carry):
        first = mm(shifted[pair], slope[pair], NT)
        second = mm(shifted[pair + 32], slope[pair + 32], NT)
        tap_buf[pair] = jnp.concatenate([first, second], axis=1).astype(BF16)
        return carry

    def taps_two(step, carry):
        taps(2 * step, 0)
        taps(2 * step + 1, 0)
        return carry

    lax.fori_loop(0, 16, taps_two, 0)
    kept = pltpu.make_async_copy(tap_buf, tt_ref, tsem)
    kept.start()
    rows_moved.wait_recv()
    rows_moved.wait_send()
    for copy in copies:
        copy.wait_send()
    stored.wait()
    kept.wait()


def rim_kernel(cin_ref, rim_ref, ck_ref, ow_ref, cot_ref, base_ref, thr_ref, gouts_ref, tapt_ref, wide):
    gx, gy = lax.axis_index("gx"), lax.axis_index("gy")
    north = (gx > 0).astype(F32)
    south = (gx < NX - 1).astype(F32)
    west = (gy > 0).astype(F32)
    east = (gy < NY - 1).astype(F32)
    value = cin_ref[...].astype(F32)
    rim = value * sigmoid(value)
    rim = rim.astype(BF16).astype(F32)
    middle = jnp.concatenate([rim_ref[0:8] * north, rim, rim_ref[8:16] * south], axis=0)
    middle = middle.reshape(18, 8, CW)
    left = jnp.concatenate(
        [rim_ref[48:49] * north, rim_ref[16:32], rim_ref[64:65] * south], axis=0
    ) * west
    right = jnp.concatenate(
        [rim_ref[56:57] * north, rim_ref[32:48], rim_ref[72:73] * south], axis=0
    ) * east
    wide[0] = jnp.concatenate([left[:, None, :], middle[:, :7]], axis=1)
    wide[1] = middle
    wide[2] = jnp.concatenate([middle[:, 1:], right[:, None, :]], axis=1)
    total = value
    for p in range(3):
        for q in range(3):
            tap = wide[q, p : p + 16].reshape(128, CW)
            number = 3 * p + q
            total = total + mm(tap.astype(BF16), ck_ref[number])
            tapt_ref[number * CW : number * CW + CW] = tap.T.astype(BF16)
    base_ref[...] = total
    gouts = (cot_ref[...].astype(F32) * (1.0 / 128.0)).astype(BF16)
    gouts_ref[...] = gouts
    thr_ref[...] = mm(gouts, ow_ref[...], NT)


def reduce_kernel(
    rows_ref, base_ref, thr_ref, gouts_ref, tapt_ref, uw_ref, ow_ref, tt_any, slot_ref, out_ref, f_ref,
    payload, half, mate, got0, got1, got2, sum1, sum2, gp2, tt_ref, slot_buf, slot_got,
    csem, psem, asem, bsem, tsem, rows_ssem, rows_rsem,
):
    gx, gy = lax.axis_index("gx"), lax.axis_index("gy")
    x, c = gx // 2, lax.rem(gx, 2)
    y, z = gy // 4, lax.rem(gy, 4)
    place = (x, y, z)

    def device(axis, index):
        where = list(place)
        where[axis] = index
        return (where[0] * 2 + c, where[1] * 4 + where[2])

    peers = [
        [lax.rem(place[axis] + step, 4) for step in (1, 2, 3)] for axis in range(3)
    ]
    other_core = (x * 2 + 1 - c, gy)
    me = gx * NY + gy
    barrier = signal_all(me)
    tt_load = pltpu.make_async_copy(tt_any, tt_ref, tsem)
    tt_load.start()
    rows = rows_ref[...].reshape(2 * NDEV, 128).astype(BF16)
    pick = (lax.broadcasted_iota(jnp.int32, (8, 128), 1) == 64).astype(BF16)
    cells = mm(pick, rows, NT)[0:1].astype(jnp.int32)
    hot = lax.broadcasted_iota(jnp.int32, (128, 2 * NDEV), 0) + 1 == cells
    hot = hot.astype(BF16)
    summed = mm(hot, rows)[:, 0:CH]
    high = summed.astype(BF16)
    rest = (summed - high.astype(F32)).astype(BF16)
    uw = uw_ref[...]
    pre = base_ref[...] + mm(high, uw) + mm(rest, uw)
    sigma = sigmoid(pre)
    active = pre * sigma
    act = active.astype(BF16)
    out_ref[...] = (pre + mm(act, ow_ref[...])).astype(BF16)
    gouts = gouts_ref[...]
    gpre = gouts.astype(F32) + thr_ref[...] * (sigma + active * (1.0 - sigma))
    gpre = gpre.astype(BF16)
    gp = mm(gpre, uw, NT)
    gp = jnp.concatenate([gp, gp], axis=1).astype(BF16)
    slot_buf[...] = mm(hot.astype(F32).T.astype(BF16), gp)[:, None, :]
    for number in range(9):
        part = mm(tapt_ref[number * CW : number * CW + CW], gpre).astype(BF16)
        payload[512 * number : 512 * number + 256] = part[:, :128]
        payload[512 * number + 256 : 512 * number + 512] = part[:, 128:]
    part = mm(active.T.astype(BF16), gouts).astype(BF16)
    payload[4608:4864] = part[:, :128]
    payload[4864:5120] = part[:, 128:]
    pooled = jnp.concatenate([summed, summed], axis=1).T[0:CH]
    pooled_high = pooled.astype(BF16)
    pooled_rest = (pooled - pooled_high.astype(F32)).astype(BF16)
    part = (mm(pooled_high, gpre) + mm(pooled_rest, gpre)).astype(BF16)
    payload[5120:5184] = part[:, :128]
    payload[5184:5248] = part[:, 128:]

    pl.semaphore_wait(barrier, NDEV - 1)

    def remote(src, dst, sems, index, target):
        copy = pltpu.make_async_remote_copy(
            src_ref=src,
            dst_ref=dst,
            send_sem=sems.at[(0,) + index],
            recv_sem=sems.at[(1,) + index],
            device_id=target,
            device_id_type=MESH,
        )
        copy.start()
        return copy

    def cross(g):
        return remote(
            payload.at[pl.ds(2048 * g + (1 - c) * 1024, 1024)],
            mate.at[pl.ds(1024 * g, 1024)],
            csem, (g,), other_core,
        )

    def tap_sums():
        hot_rows = (lax.broadcasted_iota(jnp.int32, (2 * NDEV, 128), 0) == slot_ref[...]).astype(F32)
        back_rows = slot_got[...].reshape(2 * NDEV, 128).astype(BF16)
        mine = mm(hot_rows.T.astype(BF16), back_rows)
        low = lax.broadcasted_iota(jnp.int32, (32, 128), 1) < 64
        gp2[...] = jnp.where(low, mine[0:32], mine[32:64]) * (1.0 / VOX)
        for part in range(4):
            rows = 112 if part < 3 else 128

            def add(pair, total):
                scale = gp2[pl.ds(pair, 1)]
                return total + tt_ref[pair, 112 * part : 112 * part + rows].astype(F32) * scale

            total = lax.fori_loop(0, 32, add, jnp.zeros((rows, 128), F32))
            if part == 3:
                row = lax.broadcasted_iota(jnp.int32, (128, 128), 0) - 112
                total = total * jnp.where(row > 0, 1.0 + row.astype(F32) / 16.0, 1.0)
            payload[GROWS + 112 * part : GROWS + 112 * part + rows] = total.astype(BF16)
        payload[GROWS + TROWS : PAYLOAD] = jnp.zeros((PAYLOAD - GROWS - TROWS, 128), BF16)

    got = (got0, got1, got2)
    size = (256, 64, 16)
    phase = [[None] * 3 for _ in range(3)]

    def launch(p, g, src, base):
        axis = (g + p) % 3
        out = []
        for s in range(3):
            index = peers[axis][s]
            out.append(
                remote(
                    src.at[pl.ds(base + index * size[p], size[p])],
                    got[p].at[pl.ds((3 * g + s) * size[p], size[p])],
                    psem, (p, g, s), device(axis, index),
                )
            )
        return out

    def gathered(p, g, src, base):
        axis = (g + p) % 3
        for copy in phase[p][g]:
            copy.wait_recv()
        total = src[pl.ds(base + place[axis] * size[p], size[p])].astype(F32)
        for s in range(3):
            first = (3 * g + s) * size[p]
            total = total + got[p][first : first + size[p]].astype(F32)
        return total.astype(BF16)

    def crossed(g):
        core[g].wait_recv()
        half[1024 * g : 1024 * g + 1024] = (
            payload[pl.ds(2048 * g + c * 1024, 1024)].astype(F32)
            + mate[1024 * g : 1024 * g + 1024].astype(F32)
        ).astype(BF16)
        phase[0][g] = launch(0, g, half, 1024 * g)

    def first_sum(g):
        sum1[256 * g : 256 * g + 256] = gathered(0, g, half, 1024 * g)
        phase[1][g] = launch(1, g, sum1, 256 * g)

    def second_sum(g):
        sum2[64 * g : 64 * g + 64] = gathered(1, g, sum1, 256 * g)
        phase[2][g] = launch(2, g, sum2, 64 * g)

    bases = []
    for g in range(3):
        i0, i1, i2 = place[g % 3], place[(g + 1) % 3], place[(g + 2) % 3]
        start = 2048 * g + c * 1024
        bases.append((start + i0 * 256, start + i0 * 256 + i1 * 64, start + i0 * 256 + i1 * 64 + i2 * 16))
    back = [[None] * 3 for _ in range(3)]

    def spread(p, g):
        axis = (g + p) % 3
        where = f_ref.at[pl.ds(bases[g][p], size[p])]
        back[p][g] = [
            remote(where, where, asem, (p, g, s), device(axis, peers[axis][s])) for s in range(3)
        ]

    def third_sum(g):
        f_ref[pl.ds(bases[g][2], 16)] = gathered(2, g, sum2, 64 * g)
        spread(2, g)

    def onward(p, g):
        for copy in back[p + 1][g]:
            copy.wait_recv()
        spread(p, g)

    last = []

    def across(g):
        for copy in back[0][g]:
            copy.wait_recv()
        where = f_ref.at[pl.ds(2048 * g + c * 1024, 1024)]
        last.append(remote(where, where, bsem, (g,), other_core))

    core = [cross(0), cross(1)]
    rows_moved = send_rows(me, slot_buf, slot_got, rows_ssem, rows_rsem)
    crossed(0)
    crossed(1)
    tt_load.wait()
    rows_moved.wait_recv()
    tap_sums()
    core.append(cross(2))
    first_sum(0)
    first_sum(1)
    crossed(2)
    second_sum(0)
    second_sum(1)
    first_sum(2)
    third_sum(0)
    third_sum(1)
    second_sum(2)
    onward(1, 0)
    onward(1, 1)
    third_sum(2)
    onward(0, 0)
    onward(0, 1)
    onward(1, 2)
    across(0)
    across(1)
    onward(0, 2)
    across(2)
    for copy in last:
        copy.wait_recv()
    rows_moved.wait_send()
    for copy in core + last:
        copy.wait_send()
    for p in range(3):
        for g in range(3):
            for copy in phase[p][g] + back[p][g]:
                copy.wait_send()


def result_kernel(f_ref, basis_ref, fa_ref, co_ref, fa_out, co_out, conv_ref, time_ref, up_ref, kernel_ref, out_ref, sem):
    moved = pltpu.make_async_copy(fa_ref, fa_out, sem)
    moved.start()
    co_out[...] = co_ref[...]
    for number in range(9):
        kernel_ref[number, :, :128] = f_ref[512 * number : 512 * number + 256].astype(F32)
        kernel_ref[number, :, 128:] = f_ref[512 * number + 256 : 512 * number + 512].astype(F32)
    out_ref[:, :128] = f_ref[4608:4864].astype(F32)
    out_ref[:, 128:] = f_ref[4864:5120].astype(F32)
    up_ref[:, :128] = f_ref[5120:5184].astype(F32)
    up_ref[:, 128:] = f_ref[5184:5248].astype(F32)
    tail = f_ref[GROWS : GROWS + TROWS].astype(F32)
    tail = tail + jnp.concatenate([tail[:, 64:], tail[:, :64]], axis=1)
    for k in range(7):
        block = tail[64 * k : 64 * k + 64]
        conv_ref[k] = jnp.concatenate([block, block], axis=0).T[:CH, :CH]
    row = lax.broadcasted_iota(jnp.int32, (16, 128), 0).astype(F32)
    plain = jnp.sum(tail[448:464] / (1.0 + row / 16.0), axis=0, keepdims=True) / 16.0
    column = jnp.broadcast_to(plain, (128, 128)).T[:CH, 0:1]
    time_ref[...] = column * basis_ref[...]
    moved.wait()


def time_features(timestep, channels):
    half_count = channels // 2
    frequency = jnp.exp(-math.log(10000.0) * jnp.arange(half_count, dtype=jnp.float32) / half_count)
    angles = timestep[0].astype(jnp.float32) * frequency
    return jnp.concatenate([jnp.sin(angles), jnp.cos(angles)])


def shards(
    fine_in, neighbours, parent_dev, parent_cell, timestep, conv_weight, time_weight, up_weight,
    coarse_in, coarse_kernel_in, out_weight, coarse_cot,
):
    sds = jax.ShapeDtypeStruct
    anywhere = pl.BlockSpec(memory_space=pl.ANY)
    selector = face_selector()
    basis = time_features(timestep, CH)[None, :]
    cell_lane = jnp.pad(parent_cell.astype(F32) + 1.0, (0, 64))[None, :]
    cin = coarse_in.reshape(128, CW)
    cot = coarse_cot.reshape(128, CW)

    index, source, slot = pl.pallas_call(
        route_kernel,
        out_shape=(
            sds((6, BD), jnp.int32), sds((2 * MFACE, 6), jnp.int32), sds((1, 128), jnp.int32),
        ),
        in_specs=[VMEM] * 2,
        out_specs=(VMEM,) * 3,
        name="routes",
    )(neighbours, parent_dev)

    fine_act, tt, rows_in, rim = pl.pallas_call(
        fine_kernel,
        out_shape=(
            sds((BD, CH, VOX), BF16), sds((32, TROWS, 128), BF16), sds((2 * NDEV, 1, 128), F32),
            sds((80, CW), F32),
        ),
        in_specs=[SMEM, SMEM, anywhere] + [VMEM] * 8,
        out_specs=(anywhere, anywhere, VMEM, VMEM),
        scratch_shapes=[
            pltpu.VMEM((6 * BD, 32, 128), BF16),
            pltpu.VMEM((544, 32, 128), BF16),
            pltpu.VMEM((NBUCKET * MFACE, 32, 128), BF16),
            pltpu.VMEM((80, CW), F32),
            pltpu.VMEM((BD, TROWS, VOX), BF16),
            pltpu.VMEM((BD, CH, VOX), BF16),
            pltpu.VMEM((BD, CH, VOX), BF16),
            pltpu.VMEM((32, TROWS, 128), BF16),
            pltpu.VMEM((6, 32 * STEP, 128), BF16),
            pltpu.VMEM((4, 32 * STEP, 2 * VOX), BF16),
            pltpu.VMEM((CH, 448), BF16),
            pltpu.VMEM((128, 128), F32),
            pltpu.VMEM((2 * NDEV, 1, 128), F32),
            pltpu.SemaphoreType.DMA((4,)),
            pltpu.SemaphoreType.DMA,
            pltpu.SemaphoreType.DMA,
            pltpu.SemaphoreType.DMA((20,)),
            pltpu.SemaphoreType.DMA((20,)),
            pltpu.SemaphoreType.DMA,
            pltpu.SemaphoreType.DMA,
        ],
        compiler_params=pltpu.CompilerParams(
            collective_id=0, has_side_effects=True, vmem_limit_bytes=60 * 2**20
        ),
        name="fine",
    )(
        source, index, fine_in, jnp.asarray(selector, BF16), jnp.asarray(face_spreader(selector), BF16),
        cin, conv_weight, time_weight, basis, slot, cell_lane,
    )

    base, through, gouts, tapt = pl.pallas_call(
        rim_kernel,
        out_shape=(
            sds((128, CW), F32), sds((128, CW), F32), sds((128, CW), BF16), sds((9 * CW, 128), BF16),
        ),
        in_specs=[VMEM] * 5,
        out_specs=(VMEM,) * 4,
        scratch_shapes=[pltpu.VMEM((3, 18, 8, CW), F32)],
        compiler_params=pltpu.CompilerParams(vmem_limit_bytes=32 * 2**20),
        name="rim",
    )(cin, rim, coarse_kernel_in, out_weight, cot)

    coarse_out, summed = pl.pallas_call(
        reduce_kernel,
        out_shape=(sds((128, CW), BF16), sds((PAYLOAD, 128), BF16)),
        in_specs=[VMEM] * 7 + [anywhere, VMEM],
        out_specs=(VMEM, VMEM),
        scratch_shapes=[
            pltpu.VMEM((PAYLOAD, 128), BF16),
            pltpu.VMEM((3 * 1024, 128), BF16),
            pltpu.VMEM((3 * 1024, 128), BF16),
            pltpu.VMEM((9 * 256, 128), BF16),
            pltpu.VMEM((9 * 64, 128), BF16),
            pltpu.VMEM((9 * 16, 128), BF16),
            pltpu.VMEM((3 * 256, 128), BF16),
            pltpu.VMEM((3 * 64, 128), BF16),
            pltpu.VMEM((32, 128), F32),
            pltpu.VMEM((32, TROWS, 128), BF16),
            pltpu.VMEM((2 * NDEV, 1, 128), F32),
            pltpu.VMEM((2 * NDEV, 1, 128), F32),
            pltpu.SemaphoreType.DMA((2, 3)),
            pltpu.SemaphoreType.DMA((2, 3, 3, 3)),
            pltpu.SemaphoreType.DMA((2, 3, 3, 3)),
            pltpu.SemaphoreType.DMA((2, 3)),
            pltpu.SemaphoreType.DMA,
            pltpu.SemaphoreType.DMA,
            pltpu.SemaphoreType.DMA,
        ],
        compiler_params=pltpu.CompilerParams(
            collective_id=1, has_side_effects=True, vmem_limit_bytes=48 * 2**20
        ),
        name="reduce",
    )(rows_in, base, through, gouts, tapt, up_weight, out_weight, tt, slot)

    outs = pl.pallas_call(
        result_kernel,
        out_shape=(
            sds((BD, CH, VOX), BF16), sds((128, CW), BF16),
            sds((7, CH, CH), F32), sds((CH, CH), F32), sds((CH, CW), F32), sds((9, CW, CW), F32),
            sds((CW, CW), F32),
        ),
        in_specs=[VMEM, VMEM, anywhere, VMEM],
        out_specs=(anywhere,) + (VMEM,) * 6,
        scratch_shapes=[pltpu.SemaphoreType.DMA],
        compiler_params=pltpu.CompilerParams(vmem_limit_bytes=32 * 2**20),
        name="results",
    )(summed, basis, fine_act, coarse_out)
    return (outs[0], outs[1].reshape(16, 8, CW)) + tuple(outs[2:])


def solution(mesh):
    both = ("gx", "gy")
    return jax.shard_map(
        shards,
        mesh=mesh,
        in_specs=(
            P(both, None, None), P(both, None), P(both, None), P(both), P(), P(), P(), P(),
            P("gx", "gy", None), P(), P(), P("gx", "gy", None),
        ),
        out_specs=(P(both, None, None), P("gx", "gy", None), P(), P(), P(), P(), P()),
        check_vma=False,
    )
```

```python
import math

import jax
import jax.numpy as jnp
import numpy as np
from jax import lax
from jax.experimental import pallas as pl
from jax.experimental.pallas import tpu as pltpu
from jax.sharding import PartitionSpec as P

F32 = jnp.float32
BF16 = jnp.bfloat16
MESH = pl.DeviceIdType.MESH
NDEV = 128
NX = 8
NY = 16
BD = 64
CH = 64
VOX = 512
CW = 256
MFACE = 12
NBUCKET = 12
STEP = 8
TROWS = 464
GROWS = 5248
PAYLOAD = 6144
LATE = 512
VMEM = pl.BlockSpec(memory_space=pltpu.VMEM)
SMEM = pl.BlockSpec(memory_space=pltpu.SMEM)

NN = (((1,), (0,)), ((), ()))
NT = (((1,), (1,)), ((), ()))


def mm(a, b, dims=NN):
    return lax.dot_general(a, b, dims, preferred_element_type=F32)


def sigmoid(u):
    return 0.5 * jnp.tanh(0.5 * u) + 0.5


def face_selector():
    table = np.zeros((VOX, 4 * 64), np.float32)
    for high in range(8):
        for low in range(8):
            place = 8 * high + low
            table[64 * high + 56 + low, place] = 1
            table[64 * high + low, 64 + place] = 1
            table[64 * high + 8 * low + 7, 128 + place] = 1
            table[64 * high + 8 * low, 192 + place] = 1
    return table


def face_spreader(table):
    out = np.zeros((4, 128, 2 * VOX), np.float32)
    for face in range(4):
        part = table[:, 64 * face : 64 * face + 64].T
        out[face, :64, :VOX] = part
        out[face, 64:, VOX:] = part
    return out


def bucket_offset(bucket):
    face, extra = bucket // 2, bucket % 2
    distance = 2 * (face // 2) + 1 + extra
    return distance if face % 2 == 0 else -distance


RIM_BLOCKS = (
    (0, 8, 1, 0),
    (8, 8, -1, 0),
    (16, 16, 0, 1),
    (32, 16, 0, -1),
    (48, 8, 1, 1),
    (56, 8, 1, -1),
    (64, 8, -1, 1),
    (72, 8, -1, -1),
)


def peers_of(gx, gy):
    line_x = [lax.rem(gx + step, NX) for step in range(1, NX)]
    line_y = [lax.rem(gy + step, NY) for step in range(1, NY)]
    return [(i, (i, gy)) for i in line_x], [(i, (gx, i)) for i in line_y]


def greet(devices):
    barrier = pltpu.get_barrier_semaphore()
    for other in devices:
        pl.semaphore_signal(barrier, inc=1, device_id=other, device_id_type=MESH)
    return barrier


def send_each(peers, src_of, dst, ssem, rsem):
    copies = []
    for number, (index, other) in enumerate(peers):
        copies.append(
            pltpu.make_async_remote_copy(
                src_ref=src_of(index),
                dst_ref=dst,
                send_sem=ssem.at[number],
                recv_sem=rsem.at[number],
                device_id=other,
                device_id_type=MESH,
            )
        )
        copies[-1].start()
    return copies


def route_kernel(nb_ref, own_ref, cell_in_ref, index_ref, source_ref, slot_ref, cell_ref):
    me = lax.axis_index("gx") * NY + lax.axis_index("gy")
    flat = jnp.concatenate([nb_ref[...], own_ref[...]], axis=0)
    tall = jnp.concatenate([flat.astype(F32), jnp.zeros((121, BD), F32)], axis=0)
    tall = jnp.concatenate([tall, tall], axis=1).T.astype(jnp.int32)
    blank = jnp.zeros((1, BD), F32)
    cell_ref[...] = jnp.concatenate([cell_in_ref[...].astype(F32) + 1.0, blank], axis=1)
    upper = lax.broadcasted_iota(jnp.int32, (BD, BD), 0)
    across = lax.broadcasted_iota(jnp.int32, (BD, BD), 1)
    earlier = upper < across
    slots = lax.broadcasted_iota(jnp.int32, (2 * MFACE, BD), 0)
    order = lax.broadcasted_iota(jnp.int32, (2 * MFACE, BD), 1)
    for face in range(6):
        facing = face + 1 - 2 * (face % 2)
        sign = 1 - 2 * (face % 2)
        row, column = flat[face : face + 1], tall[:BD, face : face + 1]
        holder, holder_c = row >> 6, column >> 6
        local = row & 63
        present = row >= 0
        away = present & (holder != me)
        extra = ((sign * (holder - me) + NDEV) & (NDEV - 1)) - (2 * (face // 2) + 1)
        extra = jnp.clip(extra, 0, 1)
        alike = holder_c == holder
        rank_out = jnp.sum((alike & earlier).astype(jnp.int32), axis=0, keepdims=True)
        rank_in = jnp.sum((alike & (column < row)).astype(jnp.int32), axis=0, keepdims=True)
        place = jnp.where(away, extra * MFACE + jnp.minimum(rank_out, MFACE - 1), -1)
        found = jnp.sum(jnp.where(slots == place, order, 0), axis=1, keepdims=True)
        source_ref[:, face : face + 1] = found
        far = 6 * BD + facing * (2 * MFACE) + extra * MFACE + jnp.minimum(rank_in, MFACE - 1)
        near = facing * BD + local
        index_ref[face : face + 1] = jnp.where(away, far, jnp.where(present, near, 528))
    mine, mine_c = flat[6:7], tall[:BD, 6:7]
    twin = jnp.sum(((mine == mine_c) & earlier).astype(jnp.int32), axis=0, keepdims=True)
    slot = ((mine & 15) * 8 + (mine >> 4)) * 2 + jnp.minimum(twin, 1)
    slot_ref[...] = jnp.concatenate([slot, jnp.full((1, BD), -1, jnp.int32)], axis=1)


def fine_kernel(
    src_ref, idx_ref, x_ref, sel_ref, spread_ref, cin_ref, cw_ref, tw_ref, basis_ref, slot_ref, cell_ref,
    fa_ref, tt_ref, rows_ref, rim_ref,
    own, planes, out_buf, rim_buf, shifted, slope, active_buf, tap_buf, near, spread, weight, pool, rows_buf, rows_mid,
    xsem, fsem, tsem, ssem, rsem, ysend, yrecv, xsend, xrecv,
):
    gx, gy = lax.axis_index("gx"), lax.axis_index("gy")
    me = gx * NY + gy
    loads = []
    for part in range(4):
        bricks = pl.ds(16 * part, 16)
        loads.append(
            pltpu.make_async_copy(x_ref.at[bricks], shifted.at[bricks, pl.ds(0, CH)], xsem.at[part])
        )
        loads[-1].start()
    face_to = []
    for bucket in range(NBUCKET):
        other = lax.rem(me + bucket_offset(bucket) + NDEV, NDEV)
        face_to.append((other // NY, lax.rem(other, NY)))
    rim_to = [
        (lax.rem(gx + dx + NX, NX), lax.rem(gy + dy + NY, NY)) for _, _, dx, dy in RIM_BLOCKS
    ]

    peers_x, peers_y = peers_of(gx, gy)
    partners = face_to + rim_to + [other for _, other in peers_x + peers_y]
    barrier = greet(partners)

    rim = cin_ref[...].astype(F32)
    rim = (rim * sigmoid(rim)).astype(BF16).astype(F32)
    cube = rim.reshape(16, 8, CW)
    rim_buf[0:8] = cube[15]
    rim_buf[8:16] = cube[0]
    rim_buf[16:32] = cube[:, 7, :]
    rim_buf[32:48] = cube[:, 0, :]
    rim_buf[48:56] = jnp.broadcast_to(cube[15, 7:8], (8, CW))
    rim_buf[56:64] = jnp.broadcast_to(cube[15, 0:1], (8, CW))
    rim_buf[64:72] = jnp.broadcast_to(cube[0, 7:8], (8, CW))
    rim_buf[72:80] = jnp.broadcast_to(cube[0, 0:1], (8, CW))

    low = lax.broadcasted_iota(jnp.int32, (32, 128), 1) < 64

    def flip(values):
        return jnp.concatenate([values[:, 64:], values[:, :64]], axis=1)

    def pack(values, upper):
        top, bottom = values[:32], values[32:]
        if upper:
            return jnp.where(low, flip(top), bottom)
        return jnp.where(low, top, flip(bottom))

    def extract(group, carry):
        rows = shifted[pl.ds(group * 4, 4), 0:CH].reshape(4 * CH, VOX)
        picked = mm(rows, sel_ref[...]).astype(BF16)
        for b in range(4):
            n = group * 4 + b
            brick = rows[64 * b : 64 * b + 64]
            both = picked[64 * b : 64 * b + 64]
            for face, plane in enumerate(
                (
                    pack(brick[:, 384:], True),
                    pack(brick[:, :128], False),
                    pack(both[:, :128], False),
                    pack(both[:, :128], True),
                    pack(both[:, 128:], False),
                    pack(both[:, 128:], True),
                )
            ):
                own[face * BD + n] = plane
                planes[face * BD + n] = plane
        return carry

    for part in range(4):
        loads[part].wait()
        lax.fori_loop(4 * part, 4 * part + 4, extract, 0)
    planes[528:544] = jnp.zeros((16, 32, 128), BF16)

    pl.semaphore_wait(barrier, len(partners))
    copies = []
    for face in range(6):

        def gather(slot, carry):
            out_buf[face * 2 * MFACE + slot] = own[face * BD + src_ref[slot, face]]
            return carry

        lax.fori_loop(0, 2 * MFACE, gather, 0)
        for bucket in (2 * face, 2 * face + 1):
            copies.append(
                pltpu.make_async_remote_copy(
                    src_ref=out_buf.at[pl.ds(bucket * MFACE, MFACE)],
                    dst_ref=planes.at[pl.ds(6 * BD + bucket * MFACE, MFACE)],
                    send_sem=ssem.at[bucket],
                    recv_sem=rsem.at[bucket],
                    device_id=face_to[bucket],
                    device_id_type=MESH,
                )
            )
            copies[-1].start()
    for number, (first, rows, _, _) in enumerate(RIM_BLOCKS):
        copies.append(
            pltpu.make_async_remote_copy(
                src_ref=rim_buf.at[pl.ds(first, rows)],
                dst_ref=rim_ref.at[pl.ds(first, rows)],
                send_sem=ssem.at[NBUCKET + number],
                recv_sem=rsem.at[NBUCKET + number],
                device_id=rim_to[number],
                device_id_type=MESH,
            )
        )
        copies[-1].start()

    weight[...] = jnp.concatenate([cw_ref[k] for k in range(7)], axis=1)
    pool[...] = jnp.zeros_like(pool)
    lane = lax.broadcasted_iota(jnp.int32, (CH, VOX), 1)
    by, bz = lane // 8 % 8, lane % 8
    keep = (by < 7, by > 0, bz < 7, bz > 0)
    tall_low = lax.broadcasted_iota(jnp.int32, (CH, 128), 1) < 64
    zero = jnp.zeros((CH, 128), BF16)

    def turned(values, shift):
        return jnp.concatenate([values[:, shift:], values[:, :shift]], axis=1)

    def shift_brick(n):
        field = shifted[n, 0:CH]
        flipped = turned(field, 64)
        shifted[n, 64:128, : VOX - 128] = flipped[:, : VOX - 128]
        shifted[n, 64:128, VOX - 128 :] = jnp.where(tall_low, flipped[:, VOX - 128 :], zero)
        back = turned(field, VOX - 64)
        shifted[n, 128:192, 128:] = back[:, 128:]
        shifted[n, 128:192, :128] = jnp.where(tall_low, zero, back[:, :128])
        for number, shift in enumerate((8, VOX - 8, 1, VOX - 1)):
            first = 192 + 64 * number
            moved = turned(field, shift)
            shifted[n, first : first + 64] = jnp.where(keep[number], moved, jnp.zeros_like(moved))
        shifted[n, 448:TROWS] = jnp.ones((16, VOX), BF16)

    def shift_two(pair, carry):
        shift_brick(2 * pair)
        shift_brick(2 * pair + 1)
        return carry

    lax.fori_loop(0, BD // 2, shift_two, 0)
    embed = jnp.sum(tw_ref[...] * basis_ref[...], axis=1, keepdims=True)
    pool_lane = lax.broadcasted_iota(jnp.int32, (CH, 128), 1)

    for copy in copies:
        copy.wait_recv()

    def fine_step(step, carry):
        for b in range(STEP):
            for face in range(6):
                near[face, 32 * b : 32 * b + 32] = planes[idx_ref[face, step * STEP + b]]
        for face in range(4):
            spread[face] = mm(near[2 + face], spread_ref[face]).astype(BF16)
        for b in range(STEP):
            n = step * STEP + b
            above, below = near[0, 32 * b : 32 * b + 32], near[1, 32 * b : 32 * b + 32]
            plus = jnp.concatenate([flip(above), above], axis=0)
            minus = jnp.concatenate([below, flip(below)], axis=0)
            shifted[n, 64:128, VOX - 128 :] += jnp.where(tall_low, zero, plus)
            shifted[n, 128:192, :128] += jnp.where(tall_low, minus, zero)
            for number in range(4):
                rows = spread[number, 32 * b : 32 * b + 32]
                first = 192 + 64 * number
                shifted[n, first : first + 32] += rows[:, :VOX]
                shifted[n, first + 32 : first + 64] += rows[:, VOX:]
            hidden = mm(weight[...], shifted[n, 0:448]) + embed
            sigma = sigmoid(hidden)
            active = hidden * sigma
            active_buf[n] = active.astype(BF16)
            mean = jnp.sum(active, axis=1, keepdims=True) * (1.0 / VOX)
            pool[0:64] += jnp.where(pool_lane == n, mean, 0.0)
            slope[n] = (sigma + active * (1.0 - sigma)).astype(BF16)
        return carry

    lax.fori_loop(0, BD // STEP, fine_step, 0)
    stored = pltpu.make_async_copy(active_buf, fa_ref, fsem)
    stored.start()

    pool[64:72] = jnp.broadcast_to(cell_ref[...], (8, 128))
    values = pool[...].astype(BF16)
    hot = (lax.broadcasted_iota(jnp.int32, (2 * NDEV, 128), 0) == slot_ref[...]).astype(BF16)
    rows_buf[...] = mm(hot, values, NT)[:, None, :].reshape(NY, 2 * NX, 1, 128)
    along_y = send_each(peers_y, lambda i: rows_buf.at[i], rows_mid.at[gy], ysend, yrecv)
    rows_mid[gy] = rows_buf[gy]

    def taps(pair, carry):
        first = mm(shifted[pair], slope[pair], NT)
        second = mm(shifted[pair + 32], slope[pair + 32], NT)
        tap_buf[pair] = jnp.concatenate([first, second], axis=1).astype(BF16)
        return carry

    def taps_two(step, carry):
        taps(2 * step, 0)
        taps(2 * step + 1, 0)
        return carry

    lax.fori_loop(0, 4, taps_two, 0)
    for copy in along_y:
        copy.wait_recv()
    along_x = send_each(
        peers_x, lambda i: rows_mid.at[:, pl.ds(2 * i, 2)], rows_ref.at[gx], xsend, xrecv
    )
    rows_ref[gx] = rows_mid[:, pl.ds(2 * gx, 2)]
    lax.fori_loop(4, 16, taps_two, 0)
    kept = pltpu.make_async_copy(tap_buf, tt_ref, tsem)
    kept.start()
    for copy in along_x:
        copy.wait_recv()
    for copy in along_x + along_y:
        copy.wait_send()
    for copy in copies:
        copy.wait_send()
    stored.wait()
    kept.wait()


def rim_kernel(cin_ref, rim_ref, ck_ref, ow_ref, cot_ref, base_ref, thr_ref, gouts_ref, tapt_ref, wide):
    gx, gy = lax.axis_index("gx"), lax.axis_index("gy")
    north = (gx > 0).astype(F32)
    south = (gx < NX - 1).astype(F32)
    west = (gy > 0).astype(F32)
    east = (gy < NY - 1).astype(F32)
    value = cin_ref[...].astype(F32)
    rim = value * sigmoid(value)
    rim = rim.astype(BF16).astype(F32)
    middle = jnp.concatenate([rim_ref[0:8] * north, rim, rim_ref[8:16] * south], axis=0)
    middle = middle.reshape(18, 8, CW)
    left = jnp.concatenate(
        [rim_ref[48:49] * north, rim_ref[16:32], rim_ref[64:65] * south], axis=0
    ) * west
    right = jnp.concatenate(
        [rim_ref[56:57] * north, rim_ref[32:48], rim_ref[72:73] * south], axis=0
    ) * east
    wide[0] = jnp.concatenate([left[:, None, :], middle[:, :7]], axis=1)
    wide[1] = middle
    wide[2] = jnp.concatenate([middle[:, 1:], right[:, None, :]], axis=1)
    total = value
    for p in range(3):
        for q in range(3):
            tap = wide[q, p : p + 16].reshape(128, CW)
            number = 3 * p + q
            total = total + mm(tap.astype(BF16), ck_ref[number])
            tapt_ref[number * CW : number * CW + CW] = tap.T.astype(BF16)
    base_ref[...] = total
    gouts = (cot_ref[...].astype(F32) * (1.0 / 128.0)).astype(BF16)
    gouts_ref[...] = gouts
    thr_ref[...] = mm(gouts, ow_ref[...], NT)


def reduce_kernel(
    rows_ref, base_ref, thr_ref, gouts_ref, tapt_ref, uw_ref, ow_ref, tt_any, slot_ref, out_ref, f_ref,
    payload, half, mate, got0, got1, got2, sum1, sum2, gp2, tt_ref, slot_buf, slot_mid, slot_got,
    late, late_got, late_sum, late_all, csem, psem, asem, bsem, tsem, xsend, xrecv, ysend, yrecv, lsem, lxsem, lysem,
):
    gx, gy = lax.axis_index("gx"), lax.axis_index("gy")
    x, c = gx // 2, lax.rem(gx, 2)
    y, z = gy // 4, lax.rem(gy, 4)
    place = (x, y, z)

    def device(axis, index):
        where = list(place)
        where[axis] = index
        return (where[0] * 2 + c, where[1] * 4 + where[2])

    peers = [
        [lax.rem(place[axis] + step, 4) for step in (1, 2, 3)] for axis in range(3)
    ]
    other_core = (x * 2 + 1 - c, gy)
    peers_x, peers_y = peers_of(gx, gy)
    barrier = greet([other for _, other in peers_x + peers_y])
    tt_load = pltpu.make_async_copy(tt_any, tt_ref, tsem)
    tt_load.start()
    rows = rows_ref[...].reshape(2 * NDEV, 128).astype(BF16)
    pick = (lax.broadcasted_iota(jnp.int32, (8, 128), 1) == 64).astype(BF16)
    cells = mm(pick, rows, NT)[0:1].astype(jnp.int32)
    hot = lax.broadcasted_iota(jnp.int32, (128, 2 * NDEV), 0) + 1 == cells
    hot = hot.astype(BF16)
    summed = mm(hot, rows)[:, 0:CH]
    high = summed.astype(BF16)
    rest = (summed - high.astype(F32)).astype(BF16)
    uw = uw_ref[...]
    pre = base_ref[...] + mm(high, uw) + mm(rest, uw)
    sigma = sigmoid(pre)
    active = pre * sigma
    act = active.astype(BF16)
    out_ref[...] = (pre + mm(act, ow_ref[...])).astype(BF16)
    gouts = gouts_ref[...]
    gpre = gouts.astype(F32) + thr_ref[...] * (sigma + active * (1.0 - sigma))
    gpre = gpre.astype(BF16)
    gp = mm(gpre, uw, NT)
    gp = jnp.concatenate([gp, gp], axis=1).astype(BF16)
    slot_buf[...] = mm(hot.astype(F32).T.astype(BF16), gp)[:, None, :].reshape(NX, 2 * NY, 1, 128)
    for number in range(9):
        part = mm(tapt_ref[number * CW : number * CW + CW], gpre).astype(BF16)
        payload[512 * number : 512 * number + 256] = part[:, :128]
        payload[512 * number + 256 : 512 * number + 512] = part[:, 128:]
    part = mm(active.T.astype(BF16), gouts).astype(BF16)
    payload[4608:4864] = part[:, :128]
    payload[4864:5120] = part[:, 128:]
    pooled = jnp.concatenate([summed, summed], axis=1).T[0:CH]
    pooled_high = pooled.astype(BF16)
    pooled_rest = (pooled - pooled_high.astype(F32)).astype(BF16)
    part = (mm(pooled_high, gpre) + mm(pooled_rest, gpre)).astype(BF16)
    payload[5120:5184] = part[:, :128]
    payload[5184:5248] = part[:, 128:]

    payload[GROWS:PAYLOAD] = jnp.zeros((PAYLOAD - GROWS, 128), BF16)

    pl.semaphore_wait(barrier, len(peers_x + peers_y))

    def remote(src, dst, sems, index, target):
        copy = pltpu.make_async_remote_copy(
            src_ref=src,
            dst_ref=dst,
            send_sem=sems.at[(0,) + index],
            recv_sem=sems.at[(1,) + index],
            device_id=target,
            device_id_type=MESH,
        )
        copy.start()
        return copy

    def cross(g):
        return remote(
            payload.at[pl.ds(2048 * g + (1 - c) * 1024, 1024)],
            mate.at[pl.ds(1024 * g, 1024)],
            csem, (g,), other_core,
        )

    def tap_sums():
        hot_rows = (lax.broadcasted_iota(jnp.int32, (2 * NDEV, 128), 0) == slot_ref[...]).astype(F32)
        back_rows = slot_got[...].reshape(2 * NDEV, 128).astype(BF16)
        mine = mm(hot_rows.T.astype(BF16), back_rows)
        low = lax.broadcasted_iota(jnp.int32, (32, 128), 1) < 64
        gp2[...] = jnp.where(low, mine[0:32], mine[32:64]) * (1.0 / VOX)
        for part in range(4):
            rows = 112 if part < 3 else 128

            def add(pair, total):
                scale = gp2[pl.ds(pair, 1)]
                return total + tt_ref[pair, 112 * part : 112 * part + rows].astype(F32) * scale

            total = lax.fori_loop(0, 32, add, jnp.zeros((rows, 128), F32))
            if part == 3:
                row = lax.broadcasted_iota(jnp.int32, (128, 128), 0) - 112
                total = total * jnp.where(row > 0, 1.0 + row.astype(F32) / 16.0, 1.0)
            late[112 * part : 112 * part + rows] = total.astype(BF16)
        late[TROWS:LATE] = jnp.zeros((LATE - TROWS, 128), BF16)

    got = (got0, got1, got2)
    size = (256, 64, 16)
    phase = [[None] * 3 for _ in range(3)]

    def launch(p, g, src, base):
        axis = (g + p) % 3
        out = []
        for s in range(3):
            index = peers[axis][s]
            out.append(
                remote(
                    src.at[pl.ds(base + index * size[p], size[p])],
                    got[p].at[pl.ds((3 * g + s) * size[p], size[p])],
                    psem, (p, g, s), device(axis, index),
                )
            )
        return out

    def gathered(p, g, src, base):
        axis = (g + p) % 3
        for copy in phase[p][g]:
            copy.wait_recv()
        total = src[pl.ds(base + place[axis] * size[p], size[p])].astype(F32)
        for s in range(3):
            first = (3 * g + s) * size[p]
            total = total + got[p][first : first + size[p]].astype(F32)
        return total.astype(BF16)

    def crossed(g):
        core[g].wait_recv()
        half[1024 * g : 1024 * g + 1024] = (
            payload[pl.ds(2048 * g + c * 1024, 1024)].astype(F32)
            + mate[1024 * g : 1024 * g + 1024].astype(F32)
        ).astype(BF16)
        phase[0][g] = launch(0, g, half, 1024 * g)

    def first_sum(g):
        sum1[256 * g : 256 * g + 256] = gathered(0, g, half, 1024 * g)
        phase[1][g] = launch(1, g, sum1, 256 * g)

    def second_sum(g):
        sum2[64 * g : 64 * g + 64] = gathered(1, g, sum1, 256 * g)
        phase[2][g] = launch(2, g, sum2, 64 * g)

    bases = []
    for g in range(3):
        i0, i1, i2 = place[g % 3], place[(g + 1) % 3], place[(g + 2) % 3]
        start = 2048 * g + c * 1024
        bases.append((start + i0 * 256, start + i0 * 256 + i1 * 64, start + i0 * 256 + i1 * 64 + i2 * 16))
    back = [[None] * 3 for _ in range(3)]

    def spread(p, g):
        axis = (g + p) % 3
        where = f_ref.at[pl.ds(bases[g][p], size[p])]
        back[p][g] = [
            remote(where, where, asem, (p, g, s), device(axis, peers[axis][s])) for s in range(3)
        ]

    def third_sum(g):
        f_ref[pl.ds(bases[g][2], 16)] = gathered(2, g, sum2, 64 * g)
        spread(2, g)

    def onward(p, g):
        for copy in back[p + 1][g]:
            copy.wait_recv()
        spread(p, g)

    last = []

    def across(g):
        for copy in back[0][g]:
            copy.wait_recv()
        where = f_ref.at[pl.ds(2048 * g + c * 1024, 1024)]
        last.append(remote(where, where, bsem, (g,), other_core))

    back_x = send_each(peers_x, lambda i: slot_buf.at[i], slot_mid.at[gx], xsend, xrecv)
    slot_mid[gx] = slot_buf[gx]
    core = [cross(g) for g in range(3)]
    for copy in back_x:
        copy.wait_recv()
    back_y = send_each(
        peers_y, lambda i: slot_mid.at[:, pl.ds(2 * i, 2)], slot_got.at[gy], ysend, yrecv
    )
    slot_got[gy] = slot_mid[:, pl.ds(2 * gy, 2)]
    for g in range(3):
        crossed(g)
    tt_load.wait()
    for copy in back_y:
        copy.wait_recv()
    tap_sums()
    late_y = send_each(
        peers_y, lambda i: late.at[pl.ds(32 * i, 32)], late_got.at[gy], lsem.at[0], lsem.at[1]
    )
    late_got[gy] = late[pl.ds(pl.multiple_of(32 * gy, 32), 32)]
    for g in range(3):
        first_sum(g)
    for copy in late_y:
        copy.wait_recv()
    total = late_got[0].astype(F32)
    for i in range(1, NY):
        total = total + late_got[i].astype(F32)
    late_sum[...] = total.astype(BF16)
    late_x = send_each(peers_x, lambda i: late_sum, late_all.at[gx], lxsem.at[0], lxsem.at[1])
    late_all[gx] = late_sum[...]
    for g in range(3):
        second_sum(g)
    for copy in late_x:
        copy.wait_recv()
    total = late_all[0].astype(F32)
    for i in range(1, NX):
        total = total + late_all[i].astype(F32)
    where = f_ref.at[pl.ds(pl.multiple_of(PAYLOAD + 32 * gy, 32), 32)]
    where[...] = total.astype(BF16)
    late_back = send_each(peers_y, lambda i: where, where, lysem.at[0], lysem.at[1])
    for g in range(3):
        third_sum(g)
    for p in (1, 0):
        for g in range(3):
            onward(p, g)
    for g in range(3):
        across(g)
    for copy in last + late_back:
        copy.wait_recv()
    for copy in core + last + back_x + back_y + late_y + late_x + late_back:
        copy.wait_send()
    for p in range(3):
        for g in range(3):
            for copy in phase[p][g] + back[p][g]:
                copy.wait_send()


def result_kernel(f_ref, basis_ref, fa_ref, co_ref, fa_out, co_out, conv_ref, time_ref, up_ref, kernel_ref, out_ref, sem):
    moved = pltpu.make_async_copy(fa_ref, fa_out, sem)
    moved.start()
    co_out[...] = co_ref[...]
    for number in range(9):
        kernel_ref[number, :, :128] = f_ref[512 * number : 512 * number + 256].astype(F32)
        kernel_ref[number, :, 128:] = f_ref[512 * number + 256 : 512 * number + 512].astype(F32)
    out_ref[:, :128] = f_ref[4608:4864].astype(F32)
    out_ref[:, 128:] = f_ref[4864:5120].astype(F32)
    up_ref[:, :128] = f_ref[5120:5184].astype(F32)
    up_ref[:, 128:] = f_ref[5184:5248].astype(F32)
    tail = f_ref[PAYLOAD : PAYLOAD + TROWS].astype(F32)
    tail = tail + jnp.concatenate([tail[:, 64:], tail[:, :64]], axis=1)
    for k in range(7):
        block = tail[64 * k : 64 * k + 64]
        conv_ref[k] = jnp.concatenate([block, block], axis=0).T[:CH, :CH]
    row = lax.broadcasted_iota(jnp.int32, (16, 128), 0).astype(F32)
    plain = jnp.sum(tail[448:464] / (1.0 + row / 16.0), axis=0, keepdims=True) / 16.0
    column = jnp.broadcast_to(plain, (128, 128)).T[:CH, 0:1]
    time_ref[...] = column * basis_ref[...]
    moved.wait()


def time_features(timestep, channels):
    half_count = channels // 2
    frequency = jnp.exp(-math.log(10000.0) * jnp.arange(half_count, dtype=jnp.float32) / half_count)
    angles = timestep[0].astype(jnp.float32) * frequency
    return jnp.concatenate([jnp.sin(angles), jnp.cos(angles)])


def shards(
    fine_in, neighbours, parent_dev, parent_cell, timestep, conv_weight, time_weight, up_weight,
    coarse_in, coarse_kernel_in, out_weight, coarse_cot,
):
    sds = jax.ShapeDtypeStruct
    anywhere = pl.BlockSpec(memory_space=pl.ANY)
    selector = face_selector()
    basis = time_features(timestep, CH)[None, :]
    cin = coarse_in.reshape(128, CW)
    cot = coarse_cot.reshape(128, CW)

    index, source, slot, cell_lane = pl.pallas_call(
        route_kernel,
        out_shape=(
            sds((6, BD), jnp.int32), sds((2 * MFACE, 6), jnp.int32), sds((1, 128), jnp.int32),
            sds((1, 128), F32),
        ),
        in_specs=[VMEM] * 3,
        out_specs=(VMEM,) * 4,
        name="routes",
    )(neighbours.T, parent_dev.T, parent_cell[None, :])

    fine_act, tt, rows_in, rim = pl.pallas_call(
        fine_kernel,
        out_shape=(
            sds((BD, CH, VOX), BF16), sds((32, TROWS, 128), BF16), sds((NX, NY, 2, 1, 128), F32),
            sds((80, CW), F32),
        ),
        in_specs=[SMEM, SMEM, anywhere] + [VMEM] * 8,
        out_specs=(anywhere, anywhere, VMEM, VMEM),
        scratch_shapes=[
            pltpu.VMEM((6 * BD, 32, 128), BF16),
            pltpu.VMEM((544, 32, 128), BF16),
            pltpu.VMEM((NBUCKET * MFACE, 32, 128), BF16),
            pltpu.VMEM((80, CW), F32),
            pltpu.VMEM((BD, TROWS, VOX), BF16),
            pltpu.VMEM((BD, CH, VOX), BF16),
            pltpu.VMEM((BD, CH, VOX), BF16),
            pltpu.VMEM((32, TROWS, 128), BF16),
            pltpu.VMEM((6, 32 * STEP, 128), BF16),
            pltpu.VMEM((4, 32 * STEP, 2 * VOX), BF16),
            pltpu.VMEM((CH, 448), BF16),
            pltpu.VMEM((128, 128), F32),
            pltpu.VMEM((NY, 2 * NX, 1, 128), F32),
            pltpu.VMEM((NY, 2 * NX, 1, 128), F32),
            pltpu.SemaphoreType.DMA((4,)),
            pltpu.SemaphoreType.DMA,
            pltpu.SemaphoreType.DMA,
            pltpu.SemaphoreType.DMA((20,)),
            pltpu.SemaphoreType.DMA((20,)),
            pltpu.SemaphoreType.DMA((NY - 1,)),
            pltpu.SemaphoreType.DMA((NY - 1,)),
            pltpu.SemaphoreType.DMA((NX - 1,)),
            pltpu.SemaphoreType.DMA((NX - 1,)),
        ],
        compiler_params=pltpu.CompilerParams(
            collective_id=0, has_side_effects=True, vmem_limit_bytes=55 * 2**20
        ),
        name="fine",
    )(
        source, index, fine_in, jnp.asarray(selector, BF16), jnp.asarray(face_spreader(selector), BF16),
        cin, conv_weight, time_weight, basis, slot, cell_lane,
    )

    base, through, gouts, tapt = pl.pallas_call(
        rim_kernel,
        out_shape=(
            sds((128, CW), F32), sds((128, CW), F32), sds((128, CW), BF16), sds((9 * CW, 128), BF16),
        ),
        in_specs=[VMEM] * 5,
        out_specs=(VMEM,) * 4,
        scratch_shapes=[pltpu.VMEM((3, 18, 8, CW), F32)],
        compiler_params=pltpu.CompilerParams(vmem_limit_bytes=32 * 2**20),
        name="rim",
    )(cin, rim, coarse_kernel_in, out_weight, cot)

    coarse_out, summed = pl.pallas_call(
        reduce_kernel,
        out_shape=(sds((128, CW), BF16), sds((PAYLOAD + LATE, 128), BF16)),
        in_specs=[VMEM] * 7 + [anywhere, VMEM],
        out_specs=(VMEM, VMEM),
        scratch_shapes=[
            pltpu.VMEM((PAYLOAD, 128), BF16),
            pltpu.VMEM((3 * 1024, 128), BF16),
            pltpu.VMEM((3 * 1024, 128), BF16),
            pltpu.VMEM((9 * 256, 128), BF16),
            pltpu.VMEM((9 * 64, 128), BF16),
            pltpu.VMEM((9 * 16, 128), BF16),
            pltpu.VMEM((3 * 256, 128), BF16),
            pltpu.VMEM((3 * 64, 128), BF16),
            pltpu.VMEM((32, 128), F32),
            pltpu.VMEM((32, TROWS, 128), BF16),
            pltpu.VMEM((NX, 2 * NY, 1, 128), F32),
            pltpu.VMEM((NX, 2 * NY, 1, 128), F32),
            pltpu.VMEM((NY, NX, 2, 1, 128), F32),
            pltpu.VMEM((LATE, 128), BF16),
            pltpu.VMEM((NY, 32, 128), BF16),
            pltpu.VMEM((32, 128), BF16),
            pltpu.VMEM((NX, 32, 128), BF16),
            pltpu.SemaphoreType.DMA((2, 3)),
            pltpu.SemaphoreType.DMA((2, 3, 3, 3)),
            pltpu.SemaphoreType.DMA((2, 3, 3, 3)),
            pltpu.SemaphoreType.DMA((2, 3)),
            pltpu.SemaphoreType.DMA,
            pltpu.SemaphoreType.DMA((NX - 1,)),
            pltpu.SemaphoreType.DMA((NX - 1,)),
            pltpu.SemaphoreType.DMA((NY - 1,)),
            pltpu.SemaphoreType.DMA((NY - 1,)),
            pltpu.SemaphoreType.DMA((2, NY - 1)),
            pltpu.SemaphoreType.DMA((2, NX - 1)),
            pltpu.SemaphoreType.DMA((2, NY - 1)),
        ],
        compiler_params=pltpu.CompilerParams(
            collective_id=1, has_side_effects=True, vmem_limit_bytes=48 * 2**20
        ),
        name="reduce",
    )(rows_in.reshape(2 * NDEV, 1, 128), base, through, gouts, tapt, up_weight, out_weight, tt, slot)

    outs = pl.pallas_call(
        result_kernel,
        out_shape=(
            sds((BD, CH, VOX), BF16), sds((128, CW), BF16),
            sds((7, CH, CH), F32), sds((CH, CH), F32), sds((CH, CW), F32), sds((9, CW, CW), F32),
            sds((CW, CW), F32),
        ),
        in_specs=[VMEM, VMEM, anywhere, VMEM],
        out_specs=(anywhere,) + (VMEM,) * 6,
        scratch_shapes=[pltpu.SemaphoreType.DMA],
        compiler_params=pltpu.CompilerParams(vmem_limit_bytes=32 * 2**20),
        name="results",
    )(summed, basis, fine_act, coarse_out)
    return (outs[0], outs[1].reshape(16, 8, CW)) + tuple(outs[2:])


def solution(mesh):
    both = ("gx", "gy")
    return jax.shard_map(
        shards,
        mesh=mesh,
        in_specs=(
            P(both, None, None), P(both, None), P(both, None), P(both), P(), P(), P(), P(),
            P("gx", "gy", None), P(), P(), P("gx", "gy", None),
        ),
        out_specs=(P(both, None, None), P("gx", "gy", None), P(), P(), P(), P(), P()),
        check_vma=False,
    )
```

```python
import math

import jax
import jax.numpy as jnp
import numpy as np
from jax import lax
from jax.experimental import pallas as pl
from jax.experimental.pallas import tpu as pltpu
from jax.sharding import PartitionSpec as P

F32 = jnp.float32
BF16 = jnp.bfloat16
MESH = pl.DeviceIdType.MESH
NDEV = 128
NX = 8
NY = 16
BD = 64
CH = 64
VOX = 512
CW = 256
MFACE = 12
NBUCKET = 12
STEP = 8
TROWS = 464
GROWS = 5248
PAYLOAD = 6144
LATE = 512
VMEM = pl.BlockSpec(memory_space=pltpu.VMEM)
SMEM = pl.BlockSpec(memory_space=pltpu.SMEM)

NN = (((1,), (0,)), ((), ()))
NT = (((1,), (1,)), ((), ()))


def mm(a, b, dims=NN):
    return lax.dot_general(a, b, dims, preferred_element_type=F32)


def sigmoid(u):
    return 0.5 * jnp.tanh(0.5 * u) + 0.5


def face_selector():
    table = np.zeros((VOX, 4 * 64), np.float32)
    for high in range(8):
        for low in range(8):
            place = 8 * high + low
            table[64 * high + 56 + low, place] = 1
            table[64 * high + low, 64 + place] = 1
            table[64 * high + 8 * low + 7, 128 + place] = 1
            table[64 * high + 8 * low, 192 + place] = 1
    return table


def face_spreader(table):
    out = np.zeros((4, 128, 2 * VOX), np.float32)
    for face in range(4):
        part = table[:, 64 * face : 64 * face + 64].T
        out[face, :64, :VOX] = part
        out[face, 64:, VOX:] = part
    return out


def bucket_offset(bucket):
    face, extra = bucket // 2, bucket % 2
    distance = 2 * (face // 2) + 1 + extra
    return distance if face % 2 == 0 else -distance


RIM_BLOCKS = (
    (0, 8, 1, 0),
    (8, 8, -1, 0),
    (16, 16, 0, 1),
    (32, 16, 0, -1),
    (48, 8, 1, 1),
    (56, 8, 1, -1),
    (64, 8, -1, 1),
    (72, 8, -1, -1),
)


def peers_of(gx, gy):
    line_x = [lax.rem(gx + step, NX) for step in range(1, NX)]
    line_y = [lax.rem(gy + step, NY) for step in range(1, NY)]
    return [(i, (i, gy)) for i in line_x], [(i, (gx, i)) for i in line_y]


def greet(devices):
    barrier = pltpu.get_barrier_semaphore()
    for other in devices:
        pl.semaphore_signal(barrier, inc=1, device_id=other, device_id_type=MESH)
    return barrier


def send_each(peers, src_of, dst, ssem, rsem):
    copies = []
    for number, (index, other) in enumerate(peers):
        copies.append(
            pltpu.make_async_remote_copy(
                src_ref=src_of(index),
                dst_ref=dst,
                send_sem=ssem.at[number],
                recv_sem=rsem.at[number],
                device_id=other,
                device_id_type=MESH,
            )
        )
        copies[-1].start()
    return copies


def route_kernel(nb_ref, own_ref, cell_in_ref, index_ref, source_ref, slot_ref, cell_ref):
    me = lax.axis_index("gx") * NY + lax.axis_index("gy")
    flat = jnp.concatenate([nb_ref[...], own_ref[...]], axis=0)
    tall = jnp.concatenate([flat.astype(F32), jnp.zeros((121, BD), F32)], axis=0)
    tall = jnp.concatenate([tall, tall], axis=1).T.astype(jnp.int32)
    blank = jnp.zeros((1, BD), F32)
    cell_ref[...] = jnp.concatenate([cell_in_ref[...].astype(F32) + 1.0, blank], axis=1)
    upper = lax.broadcasted_iota(jnp.int32, (BD, BD), 0)
    across = lax.broadcasted_iota(jnp.int32, (BD, BD), 1)
    earlier = upper < across
    slots = lax.broadcasted_iota(jnp.int32, (2 * MFACE, BD), 0)
    order = lax.broadcasted_iota(jnp.int32, (2 * MFACE, BD), 1)
    for face in range(6):
        facing = face + 1 - 2 * (face % 2)
        sign = 1 - 2 * (face % 2)
        row, column = flat[face : face + 1], tall[:BD, face : face + 1]
        holder, holder_c = row >> 6, column >> 6
        local = row & 63
        present = row >= 0
        away = present & (holder != me)
        extra = ((sign * (holder - me) + NDEV) & (NDEV - 1)) - (2 * (face // 2) + 1)
        extra = jnp.clip(extra, 0, 1)
        alike = holder_c == holder
        rank_out = jnp.sum((alike & earlier).astype(jnp.int32), axis=0, keepdims=True)
        rank_in = jnp.sum((alike & (column < row)).astype(jnp.int32), axis=0, keepdims=True)
        place = jnp.where(away, extra * MFACE + jnp.minimum(rank_out, MFACE - 1), -1)
        found = jnp.sum(jnp.where(slots == place, order, 0), axis=1, keepdims=True)
        source_ref[:, face : face + 1] = found
        far = 6 * BD + facing * (2 * MFACE) + extra * MFACE + jnp.minimum(rank_in, MFACE - 1)
        near = facing * BD + local
        index_ref[face : face + 1] = jnp.where(away, far, jnp.where(present, near, 528))
    mine, mine_c = flat[6:7], tall[:BD, 6:7]
    twin = jnp.sum(((mine == mine_c) & earlier).astype(jnp.int32), axis=0, keepdims=True)
    slot = ((mine & 15) * 8 + (mine >> 4)) * 2 + jnp.minimum(twin, 1)
    slot_ref[...] = jnp.concatenate([slot, jnp.full((1, BD), -1, jnp.int32)], axis=1)


def rim_pass(gx, gy, cin_ref, rim_ref, ck_ref, ow_ref, cot_ref, base_ref, thr_ref, gouts_ref, tapt_ref, wide):
    north = (gx > 0).astype(F32)
    south = (gx < NX - 1).astype(F32)
    west = (gy > 0).astype(F32)
    east = (gy < NY - 1).astype(F32)
    value = cin_ref[...].astype(F32)
    rim = value * sigmoid(value)
    rim = rim.astype(BF16).astype(F32)
    middle = jnp.concatenate([rim_ref[0:8] * north, rim, rim_ref[8:16] * south], axis=0)
    middle = middle.reshape(18, 8, CW)
    left = jnp.concatenate(
        [rim_ref[48:49] * north, rim_ref[16:32], rim_ref[64:65] * south], axis=0
    ) * west
    right = jnp.concatenate(
        [rim_ref[56:57] * north, rim_ref[32:48], rim_ref[72:73] * south], axis=0
    ) * east
    wide[0] = jnp.concatenate([left[:, None, :], middle[:, :7]], axis=1)
    wide[1] = middle
    wide[2] = jnp.concatenate([middle[:, 1:], right[:, None, :]], axis=1)
    total = value
    for p in range(3):
        for q in range(3):
            tap = wide[q, p : p + 16].reshape(128, CW)
            number = 3 * p + q
            total = total + mm(tap.astype(BF16), ck_ref[number])
            tapt_ref[number * CW : number * CW + CW] = tap.T.astype(BF16)
    base_ref[...] = total
    gouts = (cot_ref[...].astype(F32) * (1.0 / 128.0)).astype(BF16)
    gouts_ref[...] = gouts
    thr_ref[...] = mm(gouts, ow_ref[...], NT)


def step_kernel(
    src_ref, idx_ref, x_ref, ck_any, ow_any, cot_any, sel_ref, selt_ref, spread_ref, cin_ref, cw_ref,
    tw_ref, basis_ref, slot_ref, cell_ref, uw_ref,
    fa_ref, out_ref, f_ref,
    rows_ref, base_ref, thr_ref, gouts_ref, tapt_ref, rim_ref, ck_ref, ow_ref, cot_ref, wide, merged, folded, extra,
    own, planes, out_buf, rim_buf, shifted, slope, active_buf, near, spread, weight, pool, rows_buf, rows_mid,
    payload, half, mate, got0, got1, got2, sum1, sum2, gp2, slot_buf, slot_mid, slot_got,
    late, late_got, late_sum, late_all,
    xsem, wsem, fsem, ssem, rsem, ysend, yrecv, xsend, xrecv,
    csem, psem, asem, bsem, xback, yback, lsem, lxsem, lysem,
):
    gx, gy = lax.axis_index("gx"), lax.axis_index("gy")
    me = gx * NY + gy
    loads = []
    for part in range(4):
        bricks = pl.ds(16 * part, 16)
        loads.append(
            pltpu.make_async_copy(x_ref.at[bricks], shifted.at[bricks, pl.ds(0, CH)], xsem.at[part])
        )
        loads[-1].start()
    coarse_loads = [
        pltpu.make_async_copy(a, b, wsem.at[number])
        for number, (a, b) in enumerate(((ck_any, ck_ref), (ow_any, ow_ref), (cot_any, cot_ref)))
    ]
    for copy in coarse_loads:
        copy.start()
    face_to = []
    for bucket in range(NBUCKET):
        other = lax.rem(me + bucket_offset(bucket) + NDEV, NDEV)
        face_to.append((other // NY, lax.rem(other, NY)))
    rim_to = [
        (lax.rem(gx + dx + NX, NX), lax.rem(gy + dy + NY, NY)) for _, _, dx, dy in RIM_BLOCKS
    ]

    peers_x, peers_y = peers_of(gx, gy)
    partners = face_to + rim_to + [other for _, other in peers_x + peers_y]
    barrier = greet(partners)

    rim = cin_ref[...].astype(F32)
    rim = (rim * sigmoid(rim)).astype(BF16).astype(F32)
    cube = rim.reshape(16, 8, CW)
    rim_buf[0:8] = cube[15]
    rim_buf[8:16] = cube[0]
    rim_buf[16:32] = cube[:, 7, :]
    rim_buf[32:48] = cube[:, 0, :]
    rim_buf[48:56] = jnp.broadcast_to(cube[15, 7:8], (8, CW))
    rim_buf[56:64] = jnp.broadcast_to(cube[15, 0:1], (8, CW))
    rim_buf[64:72] = jnp.broadcast_to(cube[0, 7:8], (8, CW))
    rim_buf[72:80] = jnp.broadcast_to(cube[0, 0:1], (8, CW))

    low = lax.broadcasted_iota(jnp.int32, (32, 128), 1) < 64

    def flip(values):
        return jnp.concatenate([values[:, 64:], values[:, :64]], axis=1)

    def pack(values, upper):
        top, bottom = values[:32], values[32:]
        if upper:
            return jnp.where(low, flip(top), bottom)
        return jnp.where(low, top, flip(bottom))

    def extract(group, carry):
        rows = shifted[pl.ds(group * 4, 4), 0:CH].reshape(4 * CH, VOX)
        picked = mm(rows, sel_ref[...]).astype(BF16)
        for b in range(4):
            n = group * 4 + b
            brick = rows[64 * b : 64 * b + 64]
            both = picked[64 * b : 64 * b + 64]
            for face, plane in enumerate(
                (
                    pack(brick[:, 384:], True),
                    pack(brick[:, :128], False),
                    pack(both[:, :128], False),
                    pack(both[:, :128], True),
                    pack(both[:, 128:], False),
                    pack(both[:, 128:], True),
                )
            ):
                own[face * BD + n] = plane
                planes[face * BD + n] = plane
        return carry

    for part in range(4):
        loads[part].wait()
        lax.fori_loop(4 * part, 4 * part + 4, extract, 0)
    planes[528:544] = jnp.zeros((16, 32, 128), BF16)

    pl.semaphore_wait(barrier, len(partners))
    rim_copies = []
    for number, (first, rows, _, _) in enumerate(RIM_BLOCKS):
        rim_copies.append(
            pltpu.make_async_remote_copy(
                src_ref=rim_buf.at[pl.ds(first, rows)],
                dst_ref=rim_ref.at[pl.ds(first, rows)],
                send_sem=ssem.at[NBUCKET + number],
                recv_sem=rsem.at[NBUCKET + number],
                device_id=rim_to[number],
                device_id_type=MESH,
            )
        )
        rim_copies[-1].start()
    copies = []
    for face in range(6):

        def gather(slot, carry):
            out_buf[face * 2 * MFACE + slot] = own[face * BD + src_ref[slot, face]]
            return carry

        lax.fori_loop(0, 2 * MFACE, gather, 0)
        for bucket in (2 * face, 2 * face + 1):
            copies.append(
                pltpu.make_async_remote_copy(
                    src_ref=out_buf.at[pl.ds(bucket * MFACE, MFACE)],
                    dst_ref=planes.at[pl.ds(6 * BD + bucket * MFACE, MFACE)],
                    send_sem=ssem.at[bucket],
                    recv_sem=rsem.at[bucket],
                    device_id=face_to[bucket],
                    device_id_type=MESH,
                )
            )
            copies[-1].start()
    weight[...] = jnp.concatenate([cw_ref[k] for k in range(7)], axis=1)
    pool[...] = jnp.zeros_like(pool)
    embed = jnp.sum(tw_ref[...] * basis_ref[...], axis=1, keepdims=True)
    lane = lax.broadcasted_iota(jnp.int32, (CH, VOX), 1)
    by, bz = lane // 8 % 8, lane % 8
    keep = (by < 7, by > 0, bz < 7, bz > 0)
    tall_low = lax.broadcasted_iota(jnp.int32, (CH, 128), 1) < 64
    zero = jnp.zeros((CH, 128), BF16)

    def turned(values, shift):
        return jnp.concatenate([values[:, shift:], values[:, :shift]], axis=1)

    def shift_brick(n):
        field = shifted[n, 0:CH]
        flipped = turned(field, 64)
        shifted[n, 64:128, : VOX - 128] = flipped[:, : VOX - 128]
        shifted[n, 64:128, VOX - 128 :] = jnp.where(tall_low, flipped[:, VOX - 128 :], zero)
        back = turned(field, VOX - 64)
        shifted[n, 128:192, 128:] = back[:, 128:]
        shifted[n, 128:192, :128] = jnp.where(tall_low, zero, back[:, :128])
        for number, shift in enumerate((8, VOX - 8, 1, VOX - 1)):
            first = 192 + 64 * number
            moved = turned(field, shift)
            shifted[n, first : first + 64] = jnp.where(keep[number], moved, jnp.zeros_like(moved))
        shifted[n, 448:TROWS] = jnp.ones((16, VOX), BF16)
        hidden = mm(weight[...], shifted[n, 0:448]) + embed
        high = hidden.astype(BF16)
        active_buf[n] = high
        slope[n] = (hidden - high.astype(F32)).astype(BF16)

    def shift_two(pair, carry):
        shift_brick(2 * pair)
        shift_brick(2 * pair + 1)
        return carry

    lax.fori_loop(0, BD // 2, shift_two, 0)
    pool_lane = lax.broadcasted_iota(jnp.int32, (CH, 128), 1)

    for copy in coarse_loads:
        copy.wait()
    for copy in rim_copies:
        copy.wait_recv()
    rim_pass(gx, gy, cin_ref, rim_ref, ck_ref, ow_ref, cot_ref, base_ref, thr_ref, gouts_ref, tapt_ref, wide)
    for copy in copies:
        copy.wait_recv()

    def fine_step(step, carry):
        for pair in range(STEP // 2):
            n = step * STEP + 2 * pair
            lanes = slice(128 * pair, 128 * pair + 128)
            for face in range(6):
                one, two = planes[idx_ref[face, n]], planes[idx_ref[face, n + 1]]
                merged[face, 0:32, lanes] = jnp.where(low, one, flip(two))
                merged[face, 32:64, lanes] = jnp.where(low, flip(one), two)
        terms = [mm(cw_ref[1 + face], merged[face]) for face in range(6)]
        narrow = [terms[face].astype(BF16) for face in range(2, 6)]
        for pair in range(STEP // 2):
            lanes = slice(128 * pair, 128 * pair + 128)
            for half in range(2):
                one, two = narrow[2 * half][:, lanes], narrow[2 * half + 1][:, lanes]
                out = slice(128 * half, 128 * half + 128)
                folded[128 * pair : 128 * pair + 64, out] = jnp.where(tall_low, one, flip(two))
                folded[128 * pair + 64 : 128 * pair + 128, out] = jnp.where(tall_low, flip(one), two)
        extra[...] = mm(folded[...], selt_ref[...])
        for b in range(STEP):
            n = step * STEP + b
            lanes = slice(128 * (b // 2), 128 * (b // 2) + 128)
            plus, minus = terms[0][:, lanes], terms[1][:, lanes]
            plus = jnp.where(tall_low, 0.0, flip(plus) if b % 2 == 0 else plus)
            minus = jnp.where(tall_low, flip(minus) if b % 2 == 1 else minus, 0.0)
            total = jnp.zeros((CH, 128), F32)
            for j in range(4):
                part = slice(128 * j, 128 * j + 128)
                hidden = active_buf[n, :, part].astype(F32) + slope[n, :, part].astype(F32)
                hidden = hidden + extra[64 * b : 64 * b + 64, part]
                if j == 0:
                    hidden = hidden + minus
                if j == 3:
                    hidden = hidden + plus
                sigma = sigmoid(hidden)
                active = hidden * sigma
                active_buf[n, :, part] = active.astype(BF16)
                slope[n, :, part] = (sigma + active * (1.0 - sigma)).astype(BF16)
                total = total + active
            mean = jnp.sum(total, axis=1, keepdims=True) * (1.0 / VOX)
            pool[0:64] += jnp.where(pool_lane == n, mean, 0.0)
        return carry

    lax.fori_loop(0, BD // STEP, fine_step, 0)
    stored = pltpu.make_async_copy(active_buf, fa_ref, fsem)
    stored.start()

    pool[64:72] = jnp.broadcast_to(cell_ref[...], (8, 128))
    values = pool[...].astype(BF16)
    hot = (lax.broadcasted_iota(jnp.int32, (2 * NDEV, 128), 0) == slot_ref[...]).astype(BF16)
    rows_buf[...] = mm(hot, values, NT)[:, None, :].reshape(NY, 2 * NX, 1, 128)
    along_y = send_each(peers_y, lambda i: rows_buf.at[i], rows_mid.at[gy], ysend, yrecv)
    rows_mid[gy] = rows_buf[gy]

    def tap_lanes(k):
        return slice(128 * (k // 2), 128 * (k // 2) + 128)

    def tap_step(step, carry):
        bricks = [step * 2 + b % 2 + 32 * (b // 2) for b in range(4)]
        for b in range(4):
            for face in range(6):
                near[face, 32 * b : 32 * b + 32] = planes[idx_ref[face, bricks[b]]]
        for face in range(4):
            spread[face] = mm(near[2 + face], spread_ref[face]).astype(BF16)
        sums = []
        for b in range(4):
            n = bricks[b]
            above, below = near[0, 32 * b : 32 * b + 32], near[1, 32 * b : 32 * b + 32]
            plus = jnp.concatenate([flip(above), above], axis=0)
            minus = jnp.concatenate([below, flip(below)], axis=0)
            shifted[n, 64:128, VOX - 128 :] += jnp.where(tall_low, zero, plus)
            shifted[n, 128:192, :128] += jnp.where(tall_low, minus, zero)
            for number in range(4):
                rows = spread[number, 32 * b : 32 * b + 32]
                first = 192 + 64 * number
                shifted[n, first : first + 32] += rows[:, :VOX]
                shifted[n, first + 32 : first + 64] += rows[:, VOX:]
            sums.append(mm(shifted[n], slope[n], NT))
        for b in range(2):
            pair = step * 2 + b
            both = jnp.concatenate([sums[b], sums[b + 2]], axis=1).astype(BF16)
            for k in range(7):
                active_buf[2 * pair + k % 2, :, tap_lanes(k)] = both[64 * k : 64 * k + 64]
            active_buf[2 * pair + 1, 0:16, tap_lanes(7)] = both[448:TROWS]
        return carry

    def taps(first, end):
        lax.fori_loop(first, end, tap_step, 0)

    stored.wait()
    taps(0, 3)
    for copy in along_y:
        copy.wait_recv()
    along_x = send_each(
        peers_x, lambda i: rows_mid.at[:, pl.ds(2 * i, 2)], rows_ref.at[gx], xsend, xrecv
    )
    rows_ref[gx] = rows_mid[:, pl.ds(2 * gx, 2)]
    taps(3, 6)
    for copy in along_x:
        copy.wait_recv()

    x, c = gx // 2, lax.rem(gx, 2)
    y, z = gy // 4, lax.rem(gy, 4)
    place = (x, y, z)

    def device(axis, index):
        where = list(place)
        where[axis] = index
        return (where[0] * 2 + c, where[1] * 4 + where[2])

    peers = [
        [lax.rem(place[axis] + step, 4) for step in (1, 2, 3)] for axis in range(3)
    ]
    other_core = (x * 2 + 1 - c, gy)
    rows = rows_ref[...].reshape(2 * NDEV, 1, 128).reshape(2 * NDEV, 128).astype(BF16)
    pick = (lax.broadcasted_iota(jnp.int32, (8, 128), 1) == 64).astype(BF16)
    cells = mm(pick, rows, NT)[0:1].astype(jnp.int32)
    hot = lax.broadcasted_iota(jnp.int32, (128, 2 * NDEV), 0) + 1 == cells
    hot = hot.astype(BF16)
    summed = mm(hot, rows)[:, 0:CH]
    high = summed.astype(BF16)
    rest = (summed - high.astype(F32)).astype(BF16)
    uw = uw_ref[...]
    pre = base_ref[...] + mm(high, uw) + mm(rest, uw)
    sigma = sigmoid(pre)
    active = pre * sigma
    act = active.astype(BF16)
    out_ref[...] = (pre + mm(act, ow_ref[...])).astype(BF16)
    gouts = gouts_ref[...]
    gpre = gouts.astype(F32) + thr_ref[...] * (sigma + active * (1.0 - sigma))
    gpre = gpre.astype(BF16)
    gp = mm(gpre, uw, NT)
    gp = jnp.concatenate([gp, gp], axis=1).astype(BF16)
    slot_buf[...] = mm(hot.astype(F32).T.astype(BF16), gp)[:, None, :].reshape(NX, 2 * NY, 1, 128)
    for number in range(9):
        part = mm(tapt_ref[number * CW : number * CW + CW], gpre).astype(BF16)
        payload[512 * number : 512 * number + 256] = part[:, :128]
        payload[512 * number + 256 : 512 * number + 512] = part[:, 128:]
    part = mm(active.T.astype(BF16), gouts).astype(BF16)
    payload[4608:4864] = part[:, :128]
    payload[4864:5120] = part[:, 128:]
    pooled = jnp.concatenate([summed, summed], axis=1).T[0:CH]
    pooled_high = pooled.astype(BF16)
    pooled_rest = (pooled - pooled_high.astype(F32)).astype(BF16)
    part = (mm(pooled_high, gpre) + mm(pooled_rest, gpre)).astype(BF16)
    payload[5120:5184] = part[:, :128]
    payload[5184:5248] = part[:, 128:]

    payload[GROWS:PAYLOAD] = jnp.zeros((PAYLOAD - GROWS, 128), BF16)

    def remote(src, dst, sems, index, target):
        copy = pltpu.make_async_remote_copy(
            src_ref=src,
            dst_ref=dst,
            send_sem=sems.at[(0,) + index],
            recv_sem=sems.at[(1,) + index],
            device_id=target,
            device_id_type=MESH,
        )
        copy.start()
        return copy

    def cross(g):
        return remote(
            payload.at[pl.ds(2048 * g + (1 - c) * 1024, 1024)],
            mate.at[pl.ds(1024 * g, 1024)],
            csem, (g,), other_core,
        )

    def tap_sums():
        hot_rows = (lax.broadcasted_iota(jnp.int32, (2 * NDEV, 128), 0) == slot_ref[...]).astype(F32)
        back_rows = slot_got[...].reshape(2 * NDEV, 1, 128).reshape(2 * NDEV, 128).astype(BF16)
        mine = mm(hot_rows.T.astype(BF16), back_rows)
        gp2[...] = jnp.where(low, mine[0:32], mine[32:64]) * (1.0 / VOX)
        for k in range(7):

            def add(pair, total):
                block = active_buf[2 * pair + k % 2, :, tap_lanes(k)].astype(F32)
                return total + block * gp2[pl.ds(pair, 1)]

            total = lax.fori_loop(0, 32, add, jnp.zeros((CH, 128), F32), unroll=4)
            late[64 * k : 64 * k + 64] = total.astype(BF16)

        def add_plain(pair, total):
            block = active_buf[2 * pair + 1, 0:16, tap_lanes(7)].astype(F32)
            return total + block * gp2[pl.ds(pair, 1)]

        total = lax.fori_loop(0, 32, add_plain, jnp.zeros((16, 128), F32), unroll=4)
        row = lax.broadcasted_iota(jnp.int32, (16, 128), 0)
        late[448:TROWS] = (total * (1.0 + row.astype(F32) / 16.0)).astype(BF16)
        late[TROWS:LATE] = jnp.zeros((LATE - TROWS, 128), BF16)

    got = (got0, got1, got2)
    size = (256, 64, 16)
    phase = [[None] * 3 for _ in range(3)]

    def launch(p, g, src, base):
        axis = (g + p) % 3
        out = []
        for s in range(3):
            index = peers[axis][s]
            out.append(
                remote(
                    src.at[pl.ds(base + index * size[p], size[p])],
                    got[p].at[pl.ds((3 * g + s) * size[p], size[p])],
                    psem, (p, g, s), device(axis, index),
                )
            )
        return out

    def gathered(p, g, src, base):
        axis = (g + p) % 3
        for copy in phase[p][g]:
            copy.wait_recv()
        total = src[pl.ds(base + place[axis] * size[p], size[p])].astype(F32)
        for s in range(3):
            first = (3 * g + s) * size[p]
            total = total + got[p][first : first + size[p]].astype(F32)
        return total.astype(BF16)

    def crossed(g):
        core[g].wait_recv()
        half[1024 * g : 1024 * g + 1024] = (
            payload[pl.ds(2048 * g + c * 1024, 1024)].astype(F32)
            + mate[1024 * g : 1024 * g + 1024].astype(F32)
        ).astype(BF16)
        phase[0][g] = launch(0, g, half, 1024 * g)

    def first_sum(g):
        sum1[256 * g : 256 * g + 256] = gathered(0, g, half, 1024 * g)
        phase[1][g] = launch(1, g, sum1, 256 * g)

    def second_sum(g):
        sum2[64 * g : 64 * g + 64] = gathered(1, g, sum1, 256 * g)
        phase[2][g] = launch(2, g, sum2, 64 * g)

    bases = []
    for g in range(3):
        i0, i1, i2 = place[g % 3], place[(g + 1) % 3], place[(g + 2) % 3]
        start = 2048 * g + c * 1024
        bases.append((start + i0 * 256, start + i0 * 256 + i1 * 64, start + i0 * 256 + i1 * 64 + i2 * 16))
    back = [[None] * 3 for _ in range(3)]

    def share(p, g):
        axis = (g + p) % 3
        where = f_ref.at[pl.ds(bases[g][p], size[p])]
        back[p][g] = [
            remote(where, where, asem, (p, g, s), device(axis, peers[axis][s])) for s in range(3)
        ]

    def third_sum(g):
        f_ref[pl.ds(bases[g][2], 16)] = gathered(2, g, sum2, 64 * g)
        share(2, g)

    def onward(p, g):
        for copy in back[p + 1][g]:
            copy.wait_recv()
        share(p, g)

    last = []

    def across(g):
        for copy in back[0][g]:
            copy.wait_recv()
        where = f_ref.at[pl.ds(2048 * g + c * 1024, 1024)]
        last.append(remote(where, where, bsem, (g,), other_core))

    back_x = send_each(peers_x, lambda i: slot_buf.at[i], slot_mid.at[gx], xback.at[0], xback.at[1])
    slot_mid[gx] = slot_buf[gx]
    core = [cross(g) for g in range(3)]
    taps(6, 8)
    for copy in back_x:
        copy.wait_recv()
    back_y = send_each(
        peers_y, lambda i: slot_mid.at[:, pl.ds(2 * i, 2)], slot_got.at[gy], yback.at[0], yback.at[1]
    )
    slot_got[gy] = slot_mid[:, pl.ds(2 * gy, 2)]
    for g in range(3):
        crossed(g)
    taps(8, 12)
    for g in range(3):
        first_sum(g)
    taps(12, 16)
    for g in range(3):
        second_sum(g)
    for copy in back_y:
        copy.wait_recv()
    tap_sums()
    late_y = send_each(
        peers_y, lambda i: late.at[pl.ds(32 * i, 32)], late_got.at[gy], lsem.at[0], lsem.at[1]
    )
    late_got[gy] = late[pl.ds(pl.multiple_of(32 * gy, 32), 32)]
    for g in range(3):
        third_sum(g)
    for copy in late_y:
        copy.wait_recv()
    total = late_got[0].astype(F32)
    for i in range(1, NY):
        total = total + late_got[i].astype(F32)
    late_sum[...] = total.astype(BF16)
    late_x = send_each(peers_x, lambda i: late_sum, late_all.at[gx], lxsem.at[0], lxsem.at[1])
    late_all[gx] = late_sum[...]
    for g in range(3):
        onward(1, g)
    for copy in late_x:
        copy.wait_recv()
    total = late_all[0].astype(F32)
    for i in range(1, NX):
        total = total + late_all[i].astype(F32)
    where = f_ref.at[pl.ds(pl.multiple_of(PAYLOAD + 32 * gy, 32), 32)]
    where[...] = total.astype(BF16)
    late_back = send_each(peers_y, lambda i: where, where, lysem.at[0], lysem.at[1])
    for g in range(3):
        onward(0, g)
    for g in range(3):
        across(g)
    for copy in last + late_back:
        copy.wait_recv()
    for copy in core + last + along_x + along_y + copies + rim_copies + back_x + back_y + late_y + late_x + late_back:
        copy.wait_send()
    for p in range(3):
        for g in range(3):
            for copy in phase[p][g] + back[p][g]:
                copy.wait_send()


def result_kernel(f_ref, basis_ref, fa_ref, co_ref, fa_out, co_out, conv_ref, time_ref, up_ref, kernel_ref, out_ref, sem):
    moved = []
    for part in range(8):
        bricks = pl.ds(8 * part, 8)
        moved.append(pltpu.make_async_copy(fa_ref.at[bricks], fa_out.at[bricks], sem.at[part]))
        moved[-1].start()
    co_out[...] = co_ref[...]
    for number in range(9):
        kernel_ref[number, :, :128] = f_ref[512 * number : 512 * number + 256].astype(F32)
        kernel_ref[number, :, 128:] = f_ref[512 * number + 256 : 512 * number + 512].astype(F32)
    out_ref[:, :128] = f_ref[4608:4864].astype(F32)
    out_ref[:, 128:] = f_ref[4864:5120].astype(F32)
    up_ref[:, :128] = f_ref[5120:5184].astype(F32)
    up_ref[:, 128:] = f_ref[5184:5248].astype(F32)
    tail = f_ref[PAYLOAD : PAYLOAD + TROWS].astype(F32)
    tail = tail + jnp.concatenate([tail[:, 64:], tail[:, :64]], axis=1)
    for k in range(7):
        block = tail[64 * k : 64 * k + 64]
        conv_ref[k] = jnp.concatenate([block, block], axis=0).T[:CH, :CH]
    row = lax.broadcasted_iota(jnp.int32, (16, 128), 0).astype(F32)
    plain = jnp.sum(tail[448:464] / (1.0 + row / 16.0), axis=0, keepdims=True) / 16.0
    column = jnp.broadcast_to(plain, (128, 128)).T[:CH, 0:1]
    time_ref[...] = column * basis_ref[...]
    for copy in moved:
        copy.wait()


def time_features(timestep, channels):
    half_count = channels // 2
    frequency = jnp.exp(-math.log(10000.0) * jnp.arange(half_count, dtype=jnp.float32) / half_count)
    angles = timestep[0].astype(jnp.float32) * frequency
    return jnp.concatenate([jnp.sin(angles), jnp.cos(angles)])


def shards(
    fine_in, neighbours, parent_dev, parent_cell, timestep, conv_weight, time_weight, up_weight,
    coarse_in, coarse_kernel_in, out_weight, coarse_cot,
):
    sds = jax.ShapeDtypeStruct
    anywhere = pl.BlockSpec(memory_space=pl.ANY)
    selector = face_selector()
    basis = time_features(timestep, CH)[None, :]
    cin = coarse_in.reshape(128, CW)
    cot = coarse_cot.reshape(128, CW)

    index, source, slot, cell_lane = pl.pallas_call(
        route_kernel,
        out_shape=(
            sds((6, BD), jnp.int32), sds((2 * MFACE, 6), jnp.int32), sds((1, 128), jnp.int32),
            sds((1, 128), F32),
        ),
        in_specs=[VMEM] * 3,
        out_specs=(VMEM,) * 4,
        name="routes",
    )(neighbours.T, parent_dev.T, parent_cell[None, :])

    fine_act, coarse_out, summed = pl.pallas_call(
        step_kernel,
        out_shape=(
            sds((BD, CH, VOX), BF16), sds((128, CW), BF16), sds((PAYLOAD + LATE, 128), BF16),
        ),
        in_specs=[SMEM, SMEM] + [anywhere] * 4 + [VMEM] * 10,
        out_specs=(anywhere, VMEM, VMEM),
        scratch_shapes=[
            pltpu.VMEM((NX, NY, 2, 1, 128), F32),
            pltpu.VMEM((128, CW), F32),
            pltpu.VMEM((128, CW), F32),
            pltpu.VMEM((128, CW), BF16),
            pltpu.VMEM((9 * CW, 128), BF16),
            pltpu.VMEM((80, CW), F32),
            pltpu.VMEM((9, CW, CW), BF16),
            pltpu.VMEM((CW, CW), BF16),
            pltpu.VMEM((128, CW), BF16),
            pltpu.VMEM((3, 18, 8, CW), F32),
            pltpu.VMEM((6, CH, 64 * STEP), BF16),
            pltpu.VMEM((64 * STEP, 256), BF16),
            pltpu.VMEM((64 * STEP, VOX), F32),
            pltpu.VMEM((6 * BD, 32, 128), BF16),
            pltpu.VMEM((544, 32, 128), BF16),
            pltpu.VMEM((NBUCKET * MFACE, 32, 128), BF16),
            pltpu.VMEM((80, CW), F32),
            pltpu.VMEM((BD, TROWS, VOX), BF16),
            pltpu.VMEM((BD, CH, VOX), BF16),
            pltpu.VMEM((BD, CH, VOX), BF16),
            pltpu.VMEM((6, 128, 128), BF16),
            pltpu.VMEM((4, 128, 2 * VOX), BF16),
            pltpu.VMEM((CH, 448), BF16),
            pltpu.VMEM((128, 128), F32),
            pltpu.VMEM((NY, 2 * NX, 1, 128), F32),
            pltpu.VMEM((NY, 2 * NX, 1, 128), F32),
            pltpu.VMEM((PAYLOAD, 128), BF16),
            pltpu.VMEM((3 * 1024, 128), BF16),
            pltpu.VMEM((3 * 1024, 128), BF16),
            pltpu.VMEM((9 * 256, 128), BF16),
            pltpu.VMEM((9 * 64, 128), BF16),
            pltpu.VMEM((9 * 16, 128), BF16),
            pltpu.VMEM((3 * 256, 128), BF16),
            pltpu.VMEM((3 * 64, 128), BF16),
            pltpu.VMEM((32, 128), F32),
            pltpu.VMEM((NX, 2 * NY, 1, 128), F32),
            pltpu.VMEM((NX, 2 * NY, 1, 128), F32),
            pltpu.VMEM((NY, NX, 2, 1, 128), F32),
            pltpu.VMEM((LATE, 128), BF16),
            pltpu.VMEM((NY, 32, 128), BF16),
            pltpu.VMEM((32, 128), BF16),
            pltpu.VMEM((NX, 32, 128), BF16),
            pltpu.SemaphoreType.DMA((4,)),
            pltpu.SemaphoreType.DMA((3,)),
            pltpu.SemaphoreType.DMA,
            pltpu.SemaphoreType.DMA((20,)),
            pltpu.SemaphoreType.DMA((20,)),
            pltpu.SemaphoreType.DMA((NY - 1,)),
            pltpu.SemaphoreType.DMA((NY - 1,)),
            pltpu.SemaphoreType.DMA((NX - 1,)),
            pltpu.SemaphoreType.DMA((NX - 1,)),
            pltpu.SemaphoreType.DMA((2, 3)),
            pltpu.SemaphoreType.DMA((2, 3, 3, 3)),
            pltpu.SemaphoreType.DMA((2, 3, 3, 3)),
            pltpu.SemaphoreType.DMA((2, 3)),
            pltpu.SemaphoreType.DMA((2, NX - 1)),
            pltpu.SemaphoreType.DMA((2, NY - 1)),
            pltpu.SemaphoreType.DMA((2, NY - 1)),
            pltpu.SemaphoreType.DMA((2, NX - 1)),
            pltpu.SemaphoreType.DMA((2, NY - 1)),
        ],
        compiler_params=pltpu.CompilerParams(
            collective_id=0, has_side_effects=True, vmem_limit_bytes=62 * 2**20
        ),
        name="step",
    )(
        source, index, fine_in, coarse_kernel_in, out_weight, cot, jnp.asarray(selector, BF16),
        jnp.asarray(selector.T, BF16), jnp.asarray(face_spreader(selector), BF16), cin, conv_weight,
        time_weight, basis, slot, cell_lane, up_weight,
    )

    outs = pl.pallas_call(
        result_kernel,
        out_shape=(
            sds((BD, CH, VOX), BF16), sds((128, CW), BF16),
            sds((7, CH, CH), F32), sds((CH, CH), F32), sds((CH, CW), F32), sds((9, CW, CW), F32),
            sds((CW, CW), F32),
        ),
        in_specs=[VMEM, VMEM, anywhere, VMEM],
        out_specs=(anywhere,) + (VMEM,) * 6,
        scratch_shapes=[pltpu.SemaphoreType.DMA((8,))],
        compiler_params=pltpu.CompilerParams(vmem_limit_bytes=32 * 2**20),
        name="results",
    )(summed, basis, fine_act, coarse_out)
    return (outs[0], outs[1].reshape(16, 8, CW)) + tuple(outs[2:])


def solution(mesh):
    both = ("gx", "gy")
    return jax.shard_map(
        shards,
        mesh=mesh,
        in_specs=(
            P(both, None, None), P(both, None), P(both, None), P(both), P(), P(), P(), P(),
            P("gx", "gy", None), P(), P(), P("gx", "gy", None),
        ),
        out_specs=(P(both, None, None), P("gx", "gy", None), P(), P(), P(), P(), P()),
        check_vma=False,
    )
```

```python
import math

import jax
import jax.numpy as jnp
import numpy as np
from jax import lax
from jax.experimental import pallas as pl
from jax.experimental.pallas import tpu as pltpu
from jax.sharding import PartitionSpec as P

F32 = jnp.float32
BF16 = jnp.bfloat16
MESH = pl.DeviceIdType.MESH
NDEV = 128
NX = 8
NY = 16
BD = 64
CH = 64
VOX = 512
CW = 256
MFACE = 12
NBUCKET = 12
STEP = 8
TROWS = 464
GROWS = 5248
PAYLOAD = 6144
LATE = 512
VMEM = pl.BlockSpec(memory_space=pltpu.VMEM)
SMEM = pl.BlockSpec(memory_space=pltpu.SMEM)

NN = (((1,), (0,)), ((), ()))
NT = (((1,), (1,)), ((), ()))


def mm(a, b, dims=NN):
    return lax.dot_general(a, b, dims, preferred_element_type=F32)


def sigmoid(u):
    return 0.5 * jnp.tanh(0.5 * u) + 0.5


def face_selector():
    table = np.zeros((VOX, 4 * 64), np.float32)
    for high in range(8):
        for low in range(8):
            place = 8 * high + low
            table[64 * high + 56 + low, place] = 1
            table[64 * high + low, 64 + place] = 1
            table[64 * high + 8 * low + 7, 128 + place] = 1
            table[64 * high + 8 * low, 192 + place] = 1
    return table


def face_spreader(table):
    out = np.zeros((4, 128, 2 * VOX), np.float32)
    for face in range(4):
        part = table[:, 64 * face : 64 * face + 64].T
        out[face, :64, :VOX] = part
        out[face, 64:, VOX:] = part
    return out


def bucket_offset(bucket):
    face, extra = bucket // 2, bucket % 2
    distance = 2 * (face // 2) + 1 + extra
    return distance if face % 2 == 0 else -distance


RIM_BLOCKS = (
    (0, 8, 1, 0),
    (8, 8, -1, 0),
    (16, 16, 0, 1),
    (32, 16, 0, -1),
    (48, 8, 1, 1),
    (56, 8, 1, -1),
    (64, 8, -1, 1),
    (72, 8, -1, -1),
)


def peers_of(gx, gy):
    line_x = [lax.rem(gx + step, NX) for step in range(1, NX)]
    line_y = [lax.rem(gy + step, NY) for step in range(1, NY)]
    return [(i, (i, gy)) for i in line_x], [(i, (gx, i)) for i in line_y]


def greet(devices):
    barrier = pltpu.get_barrier_semaphore()
    for other in devices:
        pl.semaphore_signal(barrier, inc=1, device_id=other, device_id_type=MESH)
    return barrier


def send_each(peers, src_of, dst, ssem, rsem):
    copies = []
    for number, (index, other) in enumerate(peers):
        copies.append(
            pltpu.make_async_remote_copy(
                src_ref=src_of(index),
                dst_ref=dst,
                send_sem=ssem.at[number],
                recv_sem=rsem.at[number],
                device_id=other,
                device_id_type=MESH,
            )
        )
        copies[-1].start()
    return copies


def route_kernel(nb_ref, own_ref, cell_in_ref, index_ref, source_ref, slot_ref, cell_ref):
    me = lax.axis_index("gx") * NY + lax.axis_index("gy")
    flat = jnp.concatenate([nb_ref[...], own_ref[...]], axis=0)
    tall = jnp.concatenate([flat.astype(F32), jnp.zeros((121, BD), F32)], axis=0)
    tall = jnp.concatenate([tall, tall], axis=1).T.astype(jnp.int32)
    blank = jnp.zeros((1, BD), F32)
    cell_ref[...] = jnp.concatenate([cell_in_ref[...].astype(F32) + 1.0, blank], axis=1)
    upper = lax.broadcasted_iota(jnp.int32, (BD, BD), 0)
    across = lax.broadcasted_iota(jnp.int32, (BD, BD), 1)
    earlier = upper < across
    slots = lax.broadcasted_iota(jnp.int32, (2 * MFACE, BD), 0)
    order = lax.broadcasted_iota(jnp.int32, (2 * MFACE, BD), 1)
    for face in range(6):
        facing = face + 1 - 2 * (face % 2)
        sign = 1 - 2 * (face % 2)
        row, column = flat[face : face + 1], tall[:BD, face : face + 1]
        holder, holder_c = row >> 6, column >> 6
        local = row & 63
        present = row >= 0
        away = present & (holder != me)
        extra = ((sign * (holder - me) + NDEV) & (NDEV - 1)) - (2 * (face // 2) + 1)
        extra = jnp.clip(extra, 0, 1)
        alike = holder_c == holder
        rank_out = jnp.sum((alike & earlier).astype(jnp.int32), axis=0, keepdims=True)
        rank_in = jnp.sum((alike & (column < row)).astype(jnp.int32), axis=0, keepdims=True)
        place = jnp.where(away, extra * MFACE + jnp.minimum(rank_out, MFACE - 1), -1)
        found = jnp.sum(jnp.where(slots == place, order, 0), axis=1, keepdims=True)
        source_ref[:, face : face + 1] = found
        far = 6 * BD + facing * (2 * MFACE) + extra * MFACE + jnp.minimum(rank_in, MFACE - 1)
        near = facing * BD + local
        index_ref[face : face + 1] = jnp.where(away, far, jnp.where(present, near, 528))
    mine, mine_c = flat[6:7], tall[:BD, 6:7]
    twin = jnp.sum(((mine == mine_c) & earlier).astype(jnp.int32), axis=0, keepdims=True)
    slot = ((mine & 15) * 8 + (mine >> 4)) * 2 + jnp.minimum(twin, 1)
    slot_ref[...] = jnp.concatenate([slot, jnp.full((1, BD), -1, jnp.int32)], axis=1)


def rim_pass(gx, gy, cin_ref, rim_ref, ck_ref, ow_ref, cot_ref, base_ref, thr_ref, gouts_ref, tapt_ref, wide):
    north = (gx > 0).astype(F32)
    south = (gx < NX - 1).astype(F32)
    west = (gy > 0).astype(F32)
    east = (gy < NY - 1).astype(F32)
    value = cin_ref[...].astype(F32)
    rim = value * sigmoid(value)
    rim = rim.astype(BF16).astype(F32)
    middle = jnp.concatenate([rim_ref[0:8] * north, rim, rim_ref[8:16] * south], axis=0)
    middle = middle.reshape(18, 8, CW)
    left = jnp.concatenate(
        [rim_ref[48:49] * north, rim_ref[16:32], rim_ref[64:65] * south], axis=0
    ) * west
    right = jnp.concatenate(
        [rim_ref[56:57] * north, rim_ref[32:48], rim_ref[72:73] * south], axis=0
    ) * east
    wide[0] = jnp.concatenate([left[:, None, :], middle[:, :7]], axis=1)
    wide[1] = middle
    wide[2] = jnp.concatenate([middle[:, 1:], right[:, None, :]], axis=1)
    total = value
    for p in range(3):
        for q in range(3):
            tap = wide[q, p : p + 16].reshape(128, CW)
            number = 3 * p + q
            total = total + mm(tap.astype(BF16), ck_ref[number])
            tapt_ref[number * CW : number * CW + CW] = tap.T.astype(BF16)
    base_ref[...] = total
    gouts = (cot_ref[...].astype(F32) * (1.0 / 128.0)).astype(BF16)
    gouts_ref[...] = gouts
    thr_ref[...] = mm(gouts, ow_ref[...], NT)


def step_kernel(
    src_ref, idx_ref, x_ref, ck_any, ow_any, cot_any, sel_ref, selt_ref, spread_ref, cin_ref, cw_ref,
    tw_ref, basis_ref, slot_ref, cell_ref, uw_ref,
    fa_ref, out_ref, f_ref,
    rows_ref, base_ref, thr_ref, gouts_ref, tapt_ref, rim_ref, ck_ref, ow_ref, cot_ref, wide, merged, folded, extra,
    own, planes, out_buf, rim_buf, shifted, slope, active_buf, near, spread, weight, pool, rows_buf, rows_mid,
    payload, half, mate, got0, got1, got2, sum1, sum2, gp2, slot_buf, slot_mid, slot_got,
    late, late_got, late_sum, late_all,
    xsem, wsem, fsem, ssem, rsem, ysend, yrecv, xsend, xrecv,
    csem, psem, asem, bsem, xback, yback, lsem, lxsem, lysem,
):
    gx, gy = lax.axis_index("gx"), lax.axis_index("gy")
    me = gx * NY + gy
    loads = []
    for part in range(4):
        bricks = pl.ds(16 * part, 16)
        loads.append(
            pltpu.make_async_copy(x_ref.at[bricks], shifted.at[bricks, pl.ds(0, CH)], xsem.at[part])
        )
        loads[-1].start()
    coarse_loads = [
        pltpu.make_async_copy(a, b, wsem.at[number])
        for number, (a, b) in enumerate(((ck_any, ck_ref), (ow_any, ow_ref), (cot_any, cot_ref)))
    ]
    for copy in coarse_loads:
        copy.start()
    face_to = []
    for bucket in range(NBUCKET):
        other = lax.rem(me + bucket_offset(bucket) + NDEV, NDEV)
        face_to.append((other // NY, lax.rem(other, NY)))
    rim_to = [
        (lax.rem(gx + dx + NX, NX), lax.rem(gy + dy + NY, NY)) for _, _, dx, dy in RIM_BLOCKS
    ]

    peers_x, peers_y = peers_of(gx, gy)
    partners = face_to + rim_to + [other for _, other in peers_x + peers_y]
    barrier = greet(partners)

    rim = cin_ref[...].astype(F32)
    rim = (rim * sigmoid(rim)).astype(BF16).astype(F32)
    cube = rim.reshape(16, 8, CW)
    rim_buf[0:8] = cube[15]
    rim_buf[8:16] = cube[0]
    rim_buf[16:32] = cube[:, 7, :]
    rim_buf[32:48] = cube[:, 0, :]
    rim_buf[48:56] = jnp.broadcast_to(cube[15, 7:8], (8, CW))
    rim_buf[56:64] = jnp.broadcast_to(cube[15, 0:1], (8, CW))
    rim_buf[64:72] = jnp.broadcast_to(cube[0, 7:8], (8, CW))
    rim_buf[72:80] = jnp.broadcast_to(cube[0, 0:1], (8, CW))

    low = lax.broadcasted_iota(jnp.int32, (32, 128), 1) < 64

    def flip(values):
        return jnp.concatenate([values[:, 64:], values[:, :64]], axis=1)

    def pack(values, upper):
        top, bottom = values[:32], values[32:]
        if upper:
            return jnp.where(low, flip(top), bottom)
        return jnp.where(low, top, flip(bottom))

    def keep_plane(row, plane):
        own[row] = plane
        planes[row] = plane

    def extract_x(group, carry):
        for b in range(4):
            n = group * 4 + b
            keep_plane(n, pack(shifted[n, 0:CH, VOX - 128 :], True))
            keep_plane(BD + n, pack(shifted[n, 0:CH, :128], False))
        return carry

    def extract_yz(first):
        def body(group, carry):
            rows = shifted[pl.ds(group * 4, 4), 0:CH].reshape(4 * CH, VOX)
            lanes = slice(64 * (first - 2), 64 * (first - 2) + 128)
            picked = mm(rows, sel_ref[:, lanes]).astype(BF16)
            for b in range(4):
                n = group * 4 + b
                both = picked[64 * b : 64 * b + 64]
                keep_plane(first * BD + n, pack(both, False))
                keep_plane((first + 1) * BD + n, pack(both, True))
            return carry

        return body

    copies = []

    def send_faces(first):
        for face in (first, first + 1):

            def gather(slot, carry):
                out_buf[face * 2 * MFACE + slot] = own[face * BD + src_ref[slot, face]]
                return carry

            lax.fori_loop(0, 2 * MFACE, gather, 0, unroll=4)
            for bucket in (2 * face, 2 * face + 1):
                copies.append(
                    pltpu.make_async_remote_copy(
                        src_ref=out_buf.at[pl.ds(bucket * MFACE, MFACE)],
                        dst_ref=planes.at[pl.ds(6 * BD + bucket * MFACE, MFACE)],
                        send_sem=ssem.at[bucket],
                        recv_sem=rsem.at[bucket],
                        device_id=face_to[bucket],
                        device_id_type=MESH,
                    )
                )
                copies[-1].start()

    for part in range(4):
        loads[part].wait()
        lax.fori_loop(4 * part, 4 * part + 4, extract_x, 0)
    planes[528:544] = jnp.zeros((16, 32, 128), BF16)
    pl.semaphore_wait(barrier, len(partners))
    send_faces(0)
    lax.fori_loop(0, 16, extract_yz(4), 0)
    send_faces(4)
    lax.fori_loop(0, 16, extract_yz(2), 0)
    send_faces(2)
    rim_copies = []
    for number, (first, rows, _, _) in enumerate(RIM_BLOCKS):
        rim_copies.append(
            pltpu.make_async_remote_copy(
                src_ref=rim_buf.at[pl.ds(first, rows)],
                dst_ref=rim_ref.at[pl.ds(first, rows)],
                send_sem=ssem.at[NBUCKET + number],
                recv_sem=rsem.at[NBUCKET + number],
                device_id=rim_to[number],
                device_id_type=MESH,
            )
        )
        rim_copies[-1].start()

    weight[...] = jnp.concatenate([cw_ref[k] for k in range(7)], axis=1)
    pool[...] = jnp.zeros_like(pool)
    embed = jnp.sum(tw_ref[...] * basis_ref[...], axis=1, keepdims=True)
    lane = lax.broadcasted_iota(jnp.int32, (CH, VOX), 1)
    by, bz = lane // 8 % 8, lane % 8
    keep = (by < 7, by > 0, bz < 7, bz > 0)
    tall_low = lax.broadcasted_iota(jnp.int32, (CH, 128), 1) < 64
    zero = jnp.zeros((CH, 128), BF16)

    def turned(values, shift):
        return jnp.concatenate([values[:, shift:], values[:, :shift]], axis=1)

    def shift_brick(n):
        field = shifted[n, 0:CH]
        flipped = turned(field, 64)
        shifted[n, 64:128, : VOX - 128] = flipped[:, : VOX - 128]
        shifted[n, 64:128, VOX - 128 :] = jnp.where(tall_low, flipped[:, VOX - 128 :], zero)
        back = turned(field, VOX - 64)
        shifted[n, 128:192, 128:] = back[:, 128:]
        shifted[n, 128:192, :128] = jnp.where(tall_low, zero, back[:, :128])
        for number, shift in enumerate((8, VOX - 8, 1, VOX - 1)):
            first = 192 + 64 * number
            moved = turned(field, shift)
            shifted[n, first : first + 64] = jnp.where(keep[number], moved, jnp.zeros_like(moved))
        shifted[n, 448:TROWS] = jnp.ones((16, VOX), BF16)
        hidden = mm(weight[...], shifted[n, 0:448]) + embed
        high = hidden.astype(BF16)
        active_buf[n] = high
        slope[n] = (hidden - high.astype(F32)).astype(BF16)

    def shift_two(pair, carry):
        shift_brick(2 * pair)
        shift_brick(2 * pair + 1)
        return carry

    lax.fori_loop(0, BD // 2, shift_two, 0)
    pool_lane = lax.broadcasted_iota(jnp.int32, (CH, 128), 1)

    for copy in coarse_loads:
        copy.wait()
    for copy in rim_copies:
        copy.wait_recv()
    rim_pass(gx, gy, cin_ref, rim_ref, ck_ref, ow_ref, cot_ref, base_ref, thr_ref, gouts_ref, tapt_ref, wide)
    for copy in copies:
        copy.wait_recv()

    def fine_step(step, carry):
        for pair in range(STEP // 2):
            n = step * STEP + 2 * pair
            lanes = slice(128 * pair, 128 * pair + 128)
            for face in range(6):
                one, two = planes[idx_ref[face, n]], planes[idx_ref[face, n + 1]]
                merged[face, 0:32, lanes] = jnp.where(low, one, flip(two))
                merged[face, 32:64, lanes] = jnp.where(low, flip(one), two)
        terms = [mm(cw_ref[1 + face], merged[face]) for face in range(6)]
        narrow = [terms[face].astype(BF16) for face in range(2, 6)]
        for pair in range(STEP // 2):
            lanes = slice(128 * pair, 128 * pair + 128)
            for half in range(2):
                one, two = narrow[2 * half][:, lanes], narrow[2 * half + 1][:, lanes]
                out = slice(128 * half, 128 * half + 128)
                folded[128 * pair : 128 * pair + 64, out] = jnp.where(tall_low, one, flip(two))
                folded[128 * pair + 64 : 128 * pair + 128, out] = jnp.where(tall_low, flip(one), two)
        extra[...] = mm(folded[...], selt_ref[...])
        for b in range(STEP):
            n = step * STEP + b
            lanes = slice(128 * (b // 2), 128 * (b // 2) + 128)
            plus, minus = terms[0][:, lanes], terms[1][:, lanes]
            plus = jnp.where(tall_low, 0.0, flip(plus) if b % 2 == 0 else plus)
            minus = jnp.where(tall_low, flip(minus) if b % 2 == 1 else minus, 0.0)
            total = jnp.zeros((CH, 128), F32)
            for j in range(4):
                part = slice(128 * j, 128 * j + 128)
                hidden = active_buf[n, :, part].astype(F32) + slope[n, :, part].astype(F32)
                hidden = hidden + extra[64 * b : 64 * b + 64, part]
                if j == 0:
                    hidden = hidden + minus
                if j == 3:
                    hidden = hidden + plus
                sigma = sigmoid(hidden)
                active = hidden * sigma
                active_buf[n, :, part] = active.astype(BF16)
                slope[n, :, part] = (sigma + active * (1.0 - sigma)).astype(BF16)
                total = total + active
            mean = jnp.sum(total, axis=1, keepdims=True) * (1.0 / VOX)
            pool[0:64] += jnp.where(pool_lane == n, mean, 0.0)
        return carry

    lax.fori_loop(0, BD // STEP, fine_step, 0)
    stored = pltpu.make_async_copy(active_buf, fa_ref, fsem)
    stored.start()

    pool[64:72] = jnp.broadcast_to(cell_ref[...], (8, 128))
    values = pool[...].astype(BF16)
    hot = (lax.broadcasted_iota(jnp.int32, (2 * NDEV, 128), 0) == slot_ref[...]).astype(BF16)
    rows_buf[...] = mm(hot, values, NT)[:, None, :].reshape(NY, 2 * NX, 1, 128)
    along_y = send_each(peers_y, lambda i: rows_buf.at[i], rows_mid.at[gy], ysend, yrecv)
    rows_mid[gy] = rows_buf[gy]

    def tap_lanes(k):
        return slice(128 * (k // 2), 128 * (k // 2) + 128)

    def tap_step(step, carry):
        bricks = [step * 2 + b % 2 + 32 * (b // 2) for b in range(4)]
        for b in range(4):
            for face in range(6):
                near[face, 32 * b : 32 * b + 32] = planes[idx_ref[face, bricks[b]]]
        for face in range(4):
            spread[face] = mm(near[2 + face], spread_ref[face]).astype(BF16)
        sums = []
        for b in range(4):
            n = bricks[b]
            above, below = near[0, 32 * b : 32 * b + 32], near[1, 32 * b : 32 * b + 32]
            plus = jnp.concatenate([flip(above), above], axis=0)
            minus = jnp.concatenate([below, flip(below)], axis=0)
            shifted[n, 64:128, VOX - 128 :] += jnp.where(tall_low, zero, plus)
            shifted[n, 128:192, :128] += jnp.where(tall_low, minus, zero)
            for number in range(4):
                rows = spread[number, 32 * b : 32 * b + 32]
                first = 192 + 64 * number
                shifted[n, first : first + 32] += rows[:, :VOX]
                shifted[n, first + 32 : first + 64] += rows[:, VOX:]
            sums.append(mm(shifted[n], slope[n], NT))
        for b in range(2):
            pair = step * 2 + b
            both = jnp.concatenate([sums[b], sums[b + 2]], axis=1).astype(BF16)
            for k in range(7):
                active_buf[2 * pair + k % 2, :, tap_lanes(k)] = both[64 * k : 64 * k + 64]
            active_buf[2 * pair + 1, 0:16, tap_lanes(7)] = both[448:TROWS]
        return carry

    def taps(first, end):
        lax.fori_loop(first, end, tap_step, 0)

    stored.wait()
    taps(0, 3)
    for copy in along_y:
        copy.wait_recv()
    along_x = send_each(
        peers_x, lambda i: rows_mid.at[:, pl.ds(2 * i, 2)], rows_ref.at[gx], xsend, xrecv
    )
    rows_ref[gx] = rows_mid[:, pl.ds(2 * gx, 2)]
    taps(3, 6)
    for copy in along_x:
        copy.wait_recv()

    x, c = gx // 2, lax.rem(gx, 2)
    y, z = gy // 4, lax.rem(gy, 4)
    place = (x, y, z)

    def device(axis, index):
        where = list(place)
        where[axis] = index
        return (where[0] * 2 + c, where[1] * 4 + where[2])

    peers = [
        [lax.rem(place[axis] + step, 4) for step in (1, 2, 3)] for axis in range(3)
    ]
    other_core = (x * 2 + 1 - c, gy)
    rows = rows_ref[...].reshape(2 * NDEV, 1, 128).reshape(2 * NDEV, 128).astype(BF16)
    pick = (lax.broadcasted_iota(jnp.int32, (8, 128), 1) == 64).astype(BF16)
    cells = mm(pick, rows, NT)[0:1].astype(jnp.int32)
    hot = lax.broadcasted_iota(jnp.int32, (128, 2 * NDEV), 0) + 1 == cells
    hot = hot.astype(BF16)
    summed = mm(hot, rows)[:, 0:CH]
    high = summed.astype(BF16)
    rest = (summed - high.astype(F32)).astype(BF16)
    uw = uw_ref[...]
    pre = base_ref[...] + mm(high, uw) + mm(rest, uw)
    sigma = sigmoid(pre)
    active = pre * sigma
    act = active.astype(BF16)
    out_ref[...] = (pre + mm(act, ow_ref[...])).astype(BF16)
    gouts = gouts_ref[...]
    gpre = gouts.astype(F32) + thr_ref[...] * (sigma + active * (1.0 - sigma))
    gpre = gpre.astype(BF16)
    gp = mm(gpre, uw, NT)
    gp = jnp.concatenate([gp, gp], axis=1).astype(BF16)
    slot_buf[...] = mm(hot.astype(F32).T.astype(BF16), gp)[:, None, :].reshape(NX, 2 * NY, 1, 128)
    for number in range(9):
        part = mm(tapt_ref[number * CW : number * CW + CW], gpre).astype(BF16)
        payload[512 * number : 512 * number + 256] = part[:, :128]
        payload[512 * number + 256 : 512 * number + 512] = part[:, 128:]
    part = mm(active.T.astype(BF16), gouts).astype(BF16)
    payload[4608:4864] = part[:, :128]
    payload[4864:5120] = part[:, 128:]
    pooled = jnp.concatenate([summed, summed], axis=1).T[0:CH]
    pooled_high = pooled.astype(BF16)
    pooled_rest = (pooled - pooled_high.astype(F32)).astype(BF16)
    part = (mm(pooled_high, gpre) + mm(pooled_rest, gpre)).astype(BF16)
    payload[5120:5184] = part[:, :128]
    payload[5184:5248] = part[:, 128:]

    payload[GROWS:PAYLOAD] = jnp.zeros((PAYLOAD - GROWS, 128), BF16)

    def remote(src, dst, sems, index, target):
        copy = pltpu.make_async_remote_copy(
            src_ref=src,
            dst_ref=dst,
            send_sem=sems.at[(0,) + index],
            recv_sem=sems.at[(1,) + index],
            device_id=target,
            device_id_type=MESH,
        )
        copy.start()
        return copy

    def cross(g):
        out = []
        for s in range(4):
            index = peers[g][s] if s < 3 else place[g]
            out.append(
                remote(
                    payload.at[pl.ds(2048 * g + (1 - c) * 1024 + index * 256, 256)],
                    mate.at[pl.ds(1024 * g + index * 256, 256)],
                    csem, (g, s), other_core,
                )
            )
        return out

    def tap_sums():
        hot_rows = (lax.broadcasted_iota(jnp.int32, (2 * NDEV, 128), 0) == slot_ref[...]).astype(F32)
        back_rows = slot_got[...].reshape(2 * NDEV, 1, 128).reshape(2 * NDEV, 128).astype(BF16)
        mine = mm(hot_rows.T.astype(BF16), back_rows)
        gp2[...] = jnp.where(low, mine[0:32], mine[32:64]) * (1.0 / VOX)
        for k in range(7):

            def add(pair, total):
                block = active_buf[2 * pair + k % 2, :, tap_lanes(k)].astype(F32)
                return total + block * gp2[pl.ds(pair, 1)]

            total = lax.fori_loop(0, 32, add, jnp.zeros((CH, 128), F32), unroll=4)
            late[64 * k : 64 * k + 64] = total.astype(BF16)

        def add_plain(pair, total):
            block = active_buf[2 * pair + 1, 0:16, tap_lanes(7)].astype(F32)
            return total + block * gp2[pl.ds(pair, 1)]

        total = lax.fori_loop(0, 32, add_plain, jnp.zeros((16, 128), F32), unroll=4)
        row = lax.broadcasted_iota(jnp.int32, (16, 128), 0)
        late[448:TROWS] = (total * (1.0 + row.astype(F32) / 16.0)).astype(BF16)
        late[TROWS:LATE] = jnp.zeros((LATE - TROWS, 128), BF16)

    got = (got0, got1, got2)
    size = (256, 64, 16)
    phase = [[None] * 3 for _ in range(3)]

    def launch(p, g, src, base):
        axis = (g + p) % 3
        out = []
        for s in range(3):
            index = peers[axis][s]
            out.append(
                remote(
                    src.at[pl.ds(base + index * size[p], size[p])],
                    got[p].at[pl.ds((3 * g + s) * size[p], size[p])],
                    psem, (p, g, s), device(axis, index),
                )
            )
        return out

    def gathered(p, g, src, base):
        axis = (g + p) % 3
        for copy in phase[p][g]:
            copy.wait_recv()
        total = src[pl.ds(base + place[axis] * size[p], size[p])].astype(F32)
        for s in range(3):
            first = (3 * g + s) * size[p]
            total = total + got[p][first : first + size[p]].astype(F32)
        return total.astype(BF16)

    def crossed(g):
        phase[0][g] = []
        for s in range(4):
            index = peers[g][s] if s < 3 else place[g]
            core[g][s].wait_recv()
            mine = pl.ds(pl.multiple_of(1024 * g + index * 256, 256), 256)
            theirs = pl.ds(pl.multiple_of(2048 * g + c * 1024 + index * 256, 256), 256)
            half[mine] = (payload[theirs].astype(F32) + mate[mine].astype(F32)).astype(BF16)
            if s < 3:
                phase[0][g].append(
                    remote(
                        half.at[mine], got0.at[pl.ds((3 * g + s) * 256, 256)], psem, (0, g, s),
                        device(g, index),
                    )
                )

    def first_sum(g):
        sum1[256 * g : 256 * g + 256] = gathered(0, g, half, 1024 * g)
        phase[1][g] = launch(1, g, sum1, 256 * g)

    def second_sum(g):
        sum2[64 * g : 64 * g + 64] = gathered(1, g, sum1, 256 * g)
        phase[2][g] = launch(2, g, sum2, 64 * g)

    bases = []
    for g in range(3):
        i0, i1, i2 = place[g % 3], place[(g + 1) % 3], place[(g + 2) % 3]
        start = 2048 * g + c * 1024
        bases.append((start + i0 * 256, start + i0 * 256 + i1 * 64, start + i0 * 256 + i1 * 64 + i2 * 16))
    back = [[None] * 3 for _ in range(3)]

    def share(p, g):
        axis = (g + p) % 3
        where = f_ref.at[pl.ds(bases[g][p], size[p])]
        back[p][g] = [
            remote(where, where, asem, (p, g, s), device(axis, peers[axis][s])) for s in range(3)
        ]

    def third_sum(g):
        f_ref[pl.ds(bases[g][2], 16)] = gathered(2, g, sum2, 64 * g)
        share(2, g)

    def onward(p, g):
        for copy in back[p + 1][g]:
            copy.wait_recv()
        share(p, g)

    last = []

    def hand_over(g, s, index):
        where = f_ref.at[pl.ds(2048 * g + c * 1024 + index * 256, 256)]
        last.append(remote(where, where, bsem, (g, s), other_core))

    def across(g, s):
        back[0][g][s].wait_recv()
        hand_over(g, s, lax.rem(place[g] + 3 - s, 4))

    back_x = send_each(peers_x, lambda i: slot_buf.at[i], slot_mid.at[gx], xback.at[0], xback.at[1])
    slot_mid[gx] = slot_buf[gx]
    core = [cross(g) for g in range(3)]
    taps(6, 8)
    for copy in back_x:
        copy.wait_recv()
    back_y = send_each(
        peers_y, lambda i: slot_mid.at[:, pl.ds(2 * i, 2)], slot_got.at[gy], yback.at[0], yback.at[1]
    )
    slot_got[gy] = slot_mid[:, pl.ds(2 * gy, 2)]
    for g in range(3):
        crossed(g)
    taps(8, 12)
    for g in range(3):
        first_sum(g)
    taps(12, 16)
    for g in range(3):
        second_sum(g)
    for copy in back_y:
        copy.wait_recv()
    tap_sums()
    late_y = send_each(
        peers_y, lambda i: late.at[pl.ds(32 * i, 32)], late_got.at[gy], lsem.at[0], lsem.at[1]
    )
    late_got[gy] = late[pl.ds(pl.multiple_of(32 * gy, 32), 32)]
    for g in range(3):
        third_sum(g)
    for copy in late_y:
        copy.wait_recv()
    total = late_got[0].astype(F32)
    for i in range(1, NY):
        total = total + late_got[i].astype(F32)
    late_sum[...] = total.astype(BF16)
    late_x = send_each(peers_x, lambda i: late_sum, late_all.at[gx], lxsem.at[0], lxsem.at[1])
    late_all[gx] = late_sum[...]
    for g in range(3):
        onward(1, g)
    for copy in late_x:
        copy.wait_recv()
    total = late_all[0].astype(F32)
    for i in range(1, NX):
        total = total + late_all[i].astype(F32)
    where = f_ref.at[pl.ds(pl.multiple_of(PAYLOAD + 32 * gy, 32), 32)]
    where[...] = total.astype(BF16)
    late_back = send_each(peers_y, lambda i: where, where, lysem.at[0], lysem.at[1])
    for g in range(3):
        onward(0, g)
        hand_over(g, 3, place[g])
    for s in range(3):
        for g in range(3):
            across(g, s)
    for copy in last + late_back:
        copy.wait_recv()
    for copy in core[0] + core[1] + core[2] + last + along_x + along_y + copies + rim_copies + back_x + back_y + late_y + late_x + late_back:
        copy.wait_send()
    for p in range(3):
        for g in range(3):
            for copy in phase[p][g] + back[p][g]:
                copy.wait_send()


def result_kernel(
    f_any, basis_ref, fa_ref, co_ref, fa_out, co_out, conv_ref, time_ref, up_ref, kernel_any, out_any,
    f_ref, wide, fa_buf, co_buf, sem, fsem, ksem,
):
    loads = {}
    for part in list(range(11)) + [12]:
        rows = pl.ds(512 * part, 512)
        loads[part] = pltpu.make_async_copy(f_any.at[rows], f_ref.at[rows], fsem.at[part])
        loads[part].start()
    held = [(co_ref, co_buf, co_out)]
    for part in range(8):
        bricks = pl.ds(8 * part, 8)
        held.append((fa_ref.at[bricks], fa_buf.at[bricks], fa_out.at[bricks]))
    fetched = [
        pltpu.make_async_copy(src, buf, sem.at[0, part]) for part, (src, buf, _) in enumerate(held)
    ]
    for copy in fetched:
        copy.start()
    moved = []

    def pass_on(part):
        fetched[part].wait()
        moved.append(pltpu.make_async_copy(held[part][1], held[part][2], sem.at[1, part]))
        moved[-1].start()

    for number in range(10):
        loads[number].wait()
        wide[number, :, :128] = f_ref[512 * number : 512 * number + 256].astype(F32)
        wide[number, :, 128:] = f_ref[512 * number + 256 : 512 * number + 512].astype(F32)
        target = kernel_any.at[number] if number < 9 else out_any
        moved.append(pltpu.make_async_copy(wide.at[number], target, ksem.at[number]))
        moved[-1].start()
        if number < 9:
            pass_on(number)
    loads[10].wait()
    loads[12].wait()
    up_ref[:, :128] = f_ref[5120:5184].astype(F32)
    up_ref[:, 128:] = f_ref[5184:5248].astype(F32)
    tail = f_ref[PAYLOAD : PAYLOAD + TROWS].astype(F32)
    tail = tail + jnp.concatenate([tail[:, 64:], tail[:, :64]], axis=1)
    for k in range(7):
        block = tail[64 * k : 64 * k + 64]
        conv_ref[k] = jnp.concatenate([block, block], axis=0).T[:CH, :CH]
    row = lax.broadcasted_iota(jnp.int32, (16, 128), 0).astype(F32)
    plain = jnp.sum(tail[448:464] / (1.0 + row / 16.0), axis=0, keepdims=True) / 16.0
    column = jnp.broadcast_to(plain, (128, 128)).T[:CH, 0:1]
    time_ref[...] = column * basis_ref[...]
    for copy in moved:
        copy.wait()


def time_features(timestep, channels):
    half_count = channels // 2
    frequency = jnp.exp(-math.log(10000.0) * jnp.arange(half_count, dtype=jnp.float32) / half_count)
    angles = timestep[0].astype(jnp.float32) * frequency
    return jnp.concatenate([jnp.sin(angles), jnp.cos(angles)])


def shards(
    fine_in, neighbours, parent_dev, parent_cell, timestep, conv_weight, time_weight, up_weight,
    coarse_in, coarse_kernel_in, out_weight, coarse_cot,
):
    sds = jax.ShapeDtypeStruct
    anywhere = pl.BlockSpec(memory_space=pl.ANY)
    selector = face_selector()
    basis = time_features(timestep, CH)[None, :]
    cin = coarse_in.reshape(128, CW)
    cot = coarse_cot.reshape(128, CW)

    index, source, slot, cell_lane = pl.pallas_call(
        route_kernel,
        out_shape=(
            sds((6, BD), jnp.int32), sds((2 * MFACE, 6), jnp.int32), sds((1, 128), jnp.int32),
            sds((1, 128), F32),
        ),
        in_specs=[VMEM] * 3,
        out_specs=(VMEM,) * 4,
        name="routes",
    )(neighbours.T, parent_dev.T, parent_cell[None, :])

    fine_act, coarse_out, summed = pl.pallas_call(
        step_kernel,
        out_shape=(
            sds((BD, CH, VOX), BF16), sds((128, CW), BF16), sds((PAYLOAD + LATE, 128), BF16),
        ),
        in_specs=[SMEM, SMEM] + [anywhere] * 4 + [VMEM] * 10,
        out_specs=(anywhere, VMEM, VMEM),
        scratch_shapes=[
            pltpu.VMEM((NX, NY, 2, 1, 128), F32),
            pltpu.VMEM((128, CW), F32),
            pltpu.VMEM((128, CW), F32),
            pltpu.VMEM((128, CW), BF16),
            pltpu.VMEM((9 * CW, 128), BF16),
            pltpu.VMEM((80, CW), F32),
            pltpu.VMEM((9, CW, CW), BF16),
            pltpu.VMEM((CW, CW), BF16),
            pltpu.VMEM((128, CW), BF16),
            pltpu.VMEM((3, 18, 8, CW), F32),
            pltpu.VMEM((6, CH, 64 * STEP), BF16),
            pltpu.VMEM((64 * STEP, 256), BF16),
            pltpu.VMEM((64 * STEP, VOX), F32),
            pltpu.VMEM((6 * BD, 32, 128), BF16),
            pltpu.VMEM((544, 32, 128), BF16),
            pltpu.VMEM((NBUCKET * MFACE, 32, 128), BF16),
            pltpu.VMEM((80, CW), F32),
            pltpu.VMEM((BD, TROWS, VOX), BF16),
            pltpu.VMEM((BD, CH, VOX), BF16),
            pltpu.VMEM((BD, CH, VOX), BF16),
            pltpu.VMEM((6, 128, 128), BF16),
            pltpu.VMEM((4, 128, 2 * VOX), BF16),
            pltpu.VMEM((CH, 448), BF16),
            pltpu.VMEM((128, 128), F32),
            pltpu.VMEM((NY, 2 * NX, 1, 128), F32),
            pltpu.VMEM((NY, 2 * NX, 1, 128), F32),
            pltpu.VMEM((PAYLOAD, 128), BF16),
            pltpu.VMEM((3 * 1024, 128), BF16),
            pltpu.VMEM((3 * 1024, 128), BF16),
            pltpu.VMEM((9 * 256, 128), BF16),
            pltpu.VMEM((9 * 64, 128), BF16),
            pltpu.VMEM((9 * 16, 128), BF16),
            pltpu.VMEM((3 * 256, 128), BF16),
            pltpu.VMEM((3 * 64, 128), BF16),
            pltpu.VMEM((32, 128), F32),
            pltpu.VMEM((NX, 2 * NY, 1, 128), F32),
            pltpu.VMEM((NX, 2 * NY, 1, 128), F32),
            pltpu.VMEM((NY, NX, 2, 1, 128), F32),
            pltpu.VMEM((LATE, 128), BF16),
            pltpu.VMEM((NY, 32, 128), BF16),
            pltpu.VMEM((32, 128), BF16),
            pltpu.VMEM((NX, 32, 128), BF16),
            pltpu.SemaphoreType.DMA((4,)),
            pltpu.SemaphoreType.DMA((3,)),
            pltpu.SemaphoreType.DMA,
            pltpu.SemaphoreType.DMA((20,)),
            pltpu.SemaphoreType.DMA((20,)),
            pltpu.SemaphoreType.DMA((NY - 1,)),
            pltpu.SemaphoreType.DMA((NY - 1,)),
            pltpu.SemaphoreType.DMA((NX - 1,)),
            pltpu.SemaphoreType.DMA((NX - 1,)),
            pltpu.SemaphoreType.DMA((2, 3, 4)),
            pltpu.SemaphoreType.DMA((2, 3, 3, 3)),
            pltpu.SemaphoreType.DMA((2, 3, 3, 3)),
            pltpu.SemaphoreType.DMA((2, 3, 4)),
            pltpu.SemaphoreType.DMA((2, NX - 1)),
            pltpu.SemaphoreType.DMA((2, NY - 1)),
            pltpu.SemaphoreType.DMA((2, NY - 1)),
            pltpu.SemaphoreType.DMA((2, NX - 1)),
            pltpu.SemaphoreType.DMA((2, NY - 1)),
        ],
        compiler_params=pltpu.CompilerParams(
            collective_id=0, has_side_effects=True, vmem_limit_bytes=62 * 2**20
        ),
        name="step",
    )(
        source, index, fine_in, coarse_kernel_in, out_weight, cot, jnp.asarray(selector, BF16),
        jnp.asarray(selector.T, BF16), jnp.asarray(face_spreader(selector), BF16), cin, conv_weight,
        time_weight, basis, slot, cell_lane, up_weight,
    )

    outs = pl.pallas_call(
        result_kernel,
        out_shape=(
            sds((BD, CH, VOX), BF16), sds((128, CW), BF16),
            sds((7, CH, CH), F32), sds((CH, CH), F32), sds((CH, CW), F32), sds((9, CW, CW), F32),
            sds((CW, CW), F32),
        ),
        in_specs=[anywhere, VMEM, anywhere, anywhere],
        out_specs=(anywhere,) * 2 + (VMEM,) * 3 + (anywhere,) * 2,
        scratch_shapes=[
            pltpu.VMEM((PAYLOAD + LATE, 128), BF16),
            pltpu.VMEM((10, CW, CW), F32),
            pltpu.VMEM((BD, CH, VOX), BF16),
            pltpu.VMEM((128, CW), BF16),
            pltpu.SemaphoreType.DMA((2, 9)),
            pltpu.SemaphoreType.DMA((13,)),
            pltpu.SemaphoreType.DMA((10,)),
        ],
        compiler_params=pltpu.CompilerParams(vmem_limit_bytes=62 * 2**20),
        name="results",
    )(summed, basis, fine_act, coarse_out)
    return (outs[0], outs[1].reshape(16, 8, CW)) + tuple(outs[2:])


def solution(mesh):
    both = ("gx", "gy")
    return jax.shard_map(
        shards,
        mesh=mesh,
        in_specs=(
            P(both, None, None), P(both, None), P(both, None), P(both), P(), P(), P(), P(),
            P("gx", "gy", None), P(), P(), P("gx", "gy", None),
        ),
        out_specs=(P(both, None, None), P("gx", "gy", None), P(), P(), P(), P(), P()),
        check_vma=False,
    )
```
